32 devices in a mesh: band: 2 (over x), tile: 16 (over z, y, core).
Axes of the slice: x: 2, y: 2, z: 4, core: 2. Of those that a mesh axis runs over, the one named last changes fastest.
Arguments:
- visibilities: bfloat16 [1024, 8, 128], P(('band', 'tile')), parts along dimension 0, may hold values from -6 to 6
- screens: bfloat16 [394, 2, 8, 1024], P('band'), parts along dimension 0, may hold values from -0.9 to 1.5
- positions: float32 [197, 3], replicated, may hold values from -90 to 90
- channel_freq: float32 [128], P('band'), parts along dimension 0, may hold values from 0.9 to 1.1
- owner_tile: int32 [1024, 1], P(('band', 'tile')), parts along dimension 0, may hold values from 0 to 15; in each aligned block of 32 rows (0 to 31, 32 to 63, ...) at most 4 rows name the same one
- baseline: int32 [1024], P(('band', 'tile')), parts along dimension 0, may hold values from 0 to 19305
- time_block: int32 [1024], P(('band', 'tile')), parts along dimension 0, may hold values from 0 to 15
- row_in_tile: int32 [1024], P(('band', 'tile')), parts along dimension 0, may hold values from 0 to 31
- col_offset: int32 [1024], P(('band', 'tile')), parts along dimension 0, may hold values from 0 to 992
- valid_steps: int32 [1024], P(('band', 'tile')), parts along dimension 0, may hold values from 1 to 2
Outputs:
- grid: float32 [16, 512, 1024], P('band', 'tile'), parts along dimension 0
The draws below stay inside these ranges and needn't reach their ends.
There are 2 independent parts, one for each index of `band`. The reference program is written for one: setup_inputs(seed, part) draws one part's arguments, and reference() takes and returns one part's arrays. A program takes and returns all parts, laid end to end along the dimension named above; an argument that names none is the same for every part. Nothing has to cross between parts.
Inputs may be any that keep to these rules, and one draw needn't show every extreme that they name: `owner_tile`: in each aligned block of 32 items (the items of one device) no tile is named by more than 4 items.
All inputs are finite; a program needn't handle non-finite values.
Results may differ from the reference program's by a relative error of at most 0.0037.
Values may be sent and summed in bfloat16 or wider, within the bound.
No kernel may reach another device: no remote copies, remote signals or barrier semaphores. Data moves between devices by JAX's collectives and lax.ppermute only.
A program may use at most 128 MiB of HBM per device.

```python
import math
import jax
import jax.numpy as jnp
import numpy as np
from jax import lax

SUB = 32
CH = 64
STATIONS = 197
NT = 2
TBLK = 2
BPER = 8
ITEMS_DEV = 32
STRIP = 32
GCOLS = 1024
CAP = 4
SUBGRID_COUNT = 512
ROWS = 512
STATION_PAIRS = 19306
TIMES = 16
N_TILE = 16


def draw_screens(key, part):
    key = jax.random.fold_in(key, 11)
    key_diag, key_rest = jax.random.split(key)
    shape = (STATIONS, TBLK, 8, SUB * SUB)
    diagonal = jax.random.uniform(key_diag, shape, jnp.float32, 0.6, 1.4)
    others = 0.3 * jnp.clip(jax.random.normal(key_rest, shape, jnp.float32), -3.0, 3.0)
    entry = jnp.arange(8)[None, None, :, None]
    is_diagonal = (entry == 0) | (entry == 6)
    return jnp.where(is_diagonal, diagonal, others).astype(jnp.bfloat16)


def draw_valid_steps(key, part):
    key = jax.random.fold_in(key, 23)
    key_steps, key_spot = jax.random.split(key)
    drawn = jax.random.randint(key_steps, (SUBGRID_COUNT,), 1, NT + 1)
    chosen = jax.random.randint(key_spot, (), 0, SUBGRID_COUNT)
    return jnp.where(jnp.arange(SUBGRID_COUNT) == chosen, NT, drawn).astype(jnp.int32)


def set_ends(values, rng, smallest, largest):
    shape = values.shape
    index_at = [jax.random.randint(jax.random.fold_in(rng, axis), (), 0, shape[axis]) for axis in range(len(shape))]
    values = values.at[tuple(index_at)].set(smallest)
    longest = shape.index(max(shape))
    index_at[longest] = (index_at[longest] + 1) % shape[longest]
    return values.at[tuple(index_at)].set(largest)


def steps_of(rng, extent, cuts, least, largest):
    def one(position, shards_of):
        steps = jax.random.uniform(jax.random.fold_in(jax.random.fold_in(rng, 6), position), (shards_of,), jnp.float32, least / len(cuts), largest / len(cuts))
        return jnp.repeat(jnp.exp(steps), extent[position] // shards_of).reshape((-1,) + (1,) * (len(extent) - position - 1))

    gain = one(*cuts[0])
    for cut in cuts[1:]:
        gain = gain * one(*cut)
    return gain


def routed_block(key, own, number, rows, amount, top, bound, lean):
    sequence = jax.random.permutation(key, amount)
    packed, ordinary = shares(amount, rows * top, bound, lean, True), shares(amount, rows * top, bound, lean, False)
    places = jnp.arange(amount)

    def named(tallies, offset_by):
        used = int((tallies > 0).sum())
        fixed = max(1, used // 4)
        passed = fixed + (places - fixed + offset_by * (used - fixed)) % max(1, amount - fixed)
        return jnp.zeros((amount,), jnp.int32).at[sequence[jnp.where(places < fixed, places, passed)]].set(jnp.asarray(tallies, jnp.int32))

    tallies = jnp.where(number % 4 == 0, named(packed, number // 4), named(ordinary, number - number // 4 - 1))
    mixed = jax.random.permutation(jax.random.fold_in(own, 3), amount)
    source_of, taker = mixed[0:amount // 2 * 2:2], mixed[1:amount // 2 * 2:2]
    margin = jnp.minimum(tallies[source_of] - 1, bound - tallies[taker]) // 2
    margin = jnp.where((source_of == sequence[0]) | (taker == sequence[0]) | (tallies[taker] == 0), 0, jnp.maximum(margin, 0))
    passed = jax.random.randint(jax.random.fold_in(own, 4), (amount // 2,), 0, 1 << 20) % (margin + 1)
    tallies = tallies.at[source_of].add(-passed).at[taker].add(passed)
    items = jnp.searchsorted(jnp.cumsum(tallies), jnp.arange(rows * top), side="right").astype(jnp.int32)
    listing = items.reshape(top, rows).T
    listing = listing[jax.random.permutation(jax.random.fold_in(own, 1), rows)]
    offset_by = jax.random.randint(jax.random.fold_in(own, 2), (rows, 1), 0, top)
    return jnp.take_along_axis(listing, (jnp.arange(top)[None, :] + offset_by) % top, axis=1)


def shares(amount, total, most, skew, full):
    weights = [(1 << 20) // math.isqrt(rank ** skew) + 1 for rank in range(1, amount + 1)]
    largest = most if full else min(most, max(-(-total // amount), total * weights[0] // sum(weights)))
    least = 1 if total - largest >= amount - 1 else 0
    given, rest = [largest] + [least] * (amount - 1), total - largest - least * (amount - 1)
    while rest > 0:
        candidates = [i for i in range(1, amount) if given[i] < largest] or [i for i in range(1, amount) if given[i] < most]
        mass, remaining = sum([weights[i] for i in candidates]), rest
        for i in candidates:
            more = min(most - given[i], max(1, remaining * weights[i] // mass), rest)
            given[i] = given[i] + more
            rest = rest - more
    return np.array(given)


def normal_values(key, extent, spread, most, cuts=(), held_as=jnp.bfloat16):
    array = spread * jax.random.normal(key, extent, jnp.float32)
    if cuts:
        array = array * steps_of(key, extent, cuts, -0.22, 0.18)
    return jnp.clip(array, -most, most).astype(held_as)


def setup_inputs(seed: int = 0, part: int = 0) -> dict:
    seeds = jax.random.split(jax.random.key(seed), 11)
    own_keys = jax.random.split(jax.random.fold_in(seeds[10], part), 11)
    visibilities = normal_values(own_keys[0], (SUBGRID_COUNT, 8, NT * CH), 1.0, 6.0, ((0, 16),))
    screens = draw_screens(jax.random.fold_in(jax.random.fold_in(seeds[10], part), 71), part)
    positions = normal_values(seeds[2], (STATIONS, 3), 30.0, 90.0, (), jnp.float32)
    channel_freq = jnp.clip(jax.random.uniform(own_keys[3], (CH,), jnp.float32, 0.9, 1.1), 0.9, 1.1)
    owner_tile_keys = jax.random.split(jax.random.fold_in(own_keys[4], 1), SUBGRID_COUNT // ITEMS_DEV)
    owner_tile_turns = jax.random.permutation(jax.random.fold_in(own_keys[4], 3), SUBGRID_COUNT // ITEMS_DEV)
    owner_tile = jax.vmap(lambda own, number: routed_block(jax.random.fold_in(own_keys[4], 2), own, number, ITEMS_DEV, N_TILE, 1, CAP, 2))(owner_tile_keys, owner_tile_turns).reshape((SUBGRID_COUNT, 1))
    baseline = set_ends(jax.random.randint(own_keys[5], (SUBGRID_COUNT,), 0, STATION_PAIRS), jax.random.fold_in(own_keys[5], 1), 0, STATION_PAIRS - 1).astype(jnp.int32)
    time_block = set_ends(jax.random.randint(own_keys[6], (SUBGRID_COUNT,), 0, TIMES), jax.random.fold_in(own_keys[6], 1), 0, TIMES - 1).astype(jnp.int32)
    row_in_tile = set_ends(jax.random.randint(own_keys[7], (SUBGRID_COUNT,), 0, STRIP), jax.random.fold_in(own_keys[7], 1), 0, STRIP - 1).astype(jnp.int32)
    col_offset = set_ends(jax.random.randint(own_keys[8], (SUBGRID_COUNT,), 0, GCOLS - SUB + 1), jax.random.fold_in(own_keys[8], 1), 0, GCOLS - SUB).astype(jnp.int32)
    valid_steps = draw_valid_steps(jax.random.fold_in(jax.random.fold_in(seeds[10], part), 71), part)
    return dict(visibilities=visibilities, screens=screens, positions=positions, channel_freq=channel_freq, owner_tile=owner_tile, baseline=baseline, time_block=time_block, row_in_tile=row_in_tile, col_offset=col_offset, valid_steps=valid_steps)


hour_step = 0.003
declination = -0.5
full_circle = 2.0 * math.pi


def station_pair(baseline_ids, stations):
    series = jnp.arange(stations, dtype=jnp.int32)
    offsets = series * (2 * stations - series - 1) // 2
    station_one = jnp.sum((offsets[None, :] <= baseline_ids[:, None]).astype(jnp.int32), axis=1) - 1
    station_two = baseline_ids - station_one * (2 * stations - station_one - 1) // 2 + station_one + 1
    return station_one.astype(jnp.int32), station_two.astype(jnp.int32)


def uv_track(baseline_vec, angles):
    east_part = baseline_vec[:, 0:1]
    north_part = baseline_vec[:, 1:2]
    upward = baseline_vec[:, 2:3]
    sine_part = jnp.sin(angles)
    cosine = jnp.cos(angles)
    u_track = sine_part * east_part + cosine * north_part
    v_track = (-math.sin(declination) * cosine * east_part + math.sin(declination) * sine_part * north_part
               + math.cos(declination) * upward)
    return u_track, v_track


def phase_tables(visibilities, item_records, positions, channel_freq, stations):
    number = visibilities.shape[0]
    vis_width = NT * CH
    station_one, station_two = station_pair(item_records[:, 0], stations)
    baseline_vec = positions[station_two] - positions[station_one]
    tick_index = item_records[:, 1]
    start_time = (tick_index * NT).astype(positions.dtype)
    step_index = jnp.arange(NT).astype(positions.dtype)
    angles = hour_step * (start_time[:, None] + step_index[None, :])
    middle = hour_step * (start_time[:, None] + 0.5 * (NT - 1))
    u_now, v_now = uv_track(baseline_vec, angles)
    u_mid, v_mid = uv_track(baseline_vec, middle)
    u_delta = (u_now[:, :, None] * channel_freq[None, None, :] - u_mid[:, :, None]).reshape(number, vis_width)
    v_delta = (v_now[:, :, None] * channel_freq[None, None, :] - v_mid[:, :, None]).reshape(number, vis_width)
    live_mask = (jnp.arange(NT, dtype=jnp.int32)[None, :] < item_records[:, 4:5]).astype(positions.dtype)
    live_mask = jnp.broadcast_to(live_mask[:, :, None], (number, NT, CH)).reshape(number, vis_width)
    pixel_pos = (jnp.arange(SUB).astype(positions.dtype) - SUB // 2) / SUB
    angle_x = full_circle * pixel_pos[None, :, None] * u_delta[:, None, :]
    east_phase_table = jnp.concatenate([jnp.cos(angle_x), jnp.sin(angle_x)], axis=1).astype(jnp.bfloat16)
    angle_y = full_circle * pixel_pos[None, :, None] * v_delta[:, None, :]
    phase_real = jnp.cos(angle_y)
    phase_imag = jnp.sin(angle_y)
    samples = visibilities.astype(positions.dtype).reshape(number, 4, 2, vis_width) * live_mask[:, None, None, :]
    vis_real = samples[:, :, 0]
    vis_imag = samples[:, :, 1]
    weight_real = phase_real[:, None] * vis_real[:, :, None] - phase_imag[:, None] * vis_imag[:, :, None]
    weight_imag = phase_real[:, None] * vis_imag[:, :, None] + phase_imag[:, None] * vis_real[:, :, None]
    weighted_samples = jnp.stack([weight_real, weight_imag], axis=2).reshape(number, 8 * SUB, vis_width).astype(jnp.bfloat16)
    interval = (tick_index // BPER).astype(jnp.int32)
    return east_phase_table, weighted_samples, station_one, station_two, interval


def correct(jones_products, screens, station_one, station_two, interval):
    number = jones_products.shape[0]
    intervals = screens.shape[1]
    split_parts = jones_products.reshape(number, 2, SUB, 4, 2, SUB)
    sky_real = split_parts[:, 0, :, :, 0] - split_parts[:, 1, :, :, 1]
    sky_imag = split_parts[:, 0, :, :, 1] + split_parts[:, 1, :, :, 0]
    sky_real = jnp.transpose(sky_real, (0, 2, 1, 3)).reshape(number, 2, 2, SUB * SUB)
    sky_imag = jnp.transpose(sky_imag, (0, 2, 1, 3)).reshape(number, 2, 2, SUB * SUB)
    screen_table = screens.reshape(screens.shape[0] * intervals, 8, SUB * SUB)
    left_jones = screen_table[station_one * intervals + interval].astype(jones_products.dtype).reshape(number, 2, 2, 2, SUB * SUB)
    right_jones = screen_table[station_two * intervals + interval].astype(jones_products.dtype).reshape(number, 2, 2, 2, SUB * SUB)
    left_real = left_jones[:, :, :, 0]
    left_imag = left_jones[:, :, :, 1]
    right_real = right_jones[:, :, :, 0]
    right_imag = right_jones[:, :, :, 1]
    mixed_real = jnp.sum(left_real[:, :, :, None] * sky_real[:, None] - left_imag[:, :, :, None] * sky_imag[:, None], axis=2)
    mixed_imag = jnp.sum(left_real[:, :, :, None] * sky_imag[:, None] + left_imag[:, :, :, None] * sky_real[:, None], axis=2)
    out_real = jnp.sum(mixed_real[:, :, None] * right_real[:, None] + mixed_imag[:, :, None] * right_imag[:, None], axis=3)
    out_imag = jnp.sum(mixed_imag[:, :, None] * right_real[:, None] - mixed_real[:, :, None] * right_imag[:, None], axis=3)
    return out_real.reshape(number, 4, SUB, SUB), out_imag.reshape(number, 4, SUB, SUB)


def place(grid_acc, subgrids, row_start, col_start):
    number = subgrids.shape[0]
    values = jnp.transpose(subgrids.reshape(number, 8, SUB, SUB), (1, 0, 2, 3))
    offsets = jnp.arange(SUB, dtype=jnp.int32)
    row_index = row_start[:, None, None] + offsets[None, :, None]
    col_index = col_start[:, None, None] + offsets[None, None, :]
    return grid_acc.at[:, row_index, col_index].add(values)


def reference(visibilities, screens, positions, channel_freq, owner_tile, baseline, time_block, row_in_tile, col_offset, valid_steps):
    item_records = jnp.stack([baseline, time_block, owner_tile[:, 0] * STRIP + row_in_tile, col_offset, valid_steps], axis=1).astype(jnp.int32)
    block_count = SUBGRID_COUNT // ITEMS_DEV
    vis_blocks = visibilities.reshape(block_count, ITEMS_DEV, 8, NT * CH)
    meta_blocks = item_records.reshape(block_count, ITEMS_DEV, 5)
    stations = screens.shape[0]

    def advance(padded, block_data):
        vis_block, meta_block = block_data
        east_phase_table, weighted_samples, station_one, station_two, interval = phase_tables(vis_block, meta_block, positions, channel_freq, stations)
        jones_products = jnp.einsum('qdg,qrg->qdr', east_phase_table.astype(jnp.float32), weighted_samples.astype(jnp.float32),
                              precision=lax.Precision.HIGHEST)
        real_part, imag_part = correct(jones_products, screens, station_one, station_two, interval)
        spectrum = jnp.fft.fft2(real_part + 1j * imag_part)
        subgrids = jnp.stack([jnp.real(spectrum), jnp.imag(spectrum)], axis=2).reshape(ITEMS_DEV, 8, SUB * SUB) / (SUB * SUB)
        padded = place(padded, subgrids, meta_block[:, 2], meta_block[:, 3])
        return padded, None

    padded = jnp.zeros((8, ROWS + SUB, GCOLS), jnp.float32)
    padded, unused = lax.scan(advance, padded, (vis_blocks, meta_blocks))
    return padded[:, SUB // 2:SUB // 2 + ROWS]
```

```python
import functools
import math

import jax
import jax.numpy as jnp
import numpy as np
from jax import lax
from jax.experimental import pallas as pl
from jax.experimental.pallas import tpu as pltpu
from jax.sharding import PartitionSpec as P

SUB = 32
NT = 2
BPER = 8
STRIP = 32
HALF = 16
LANES = 128
KINDS = 48

hour_step = 0.003
declination = -0.5

F32 = jnp.float32
BF16 = jnp.bfloat16
VMEM = pl.BlockSpec(memory_space=pltpu.VMEM)
SMEM = pl.BlockSpec(memory_space=pltpu.SMEM)
ANY = pl.BlockSpec(memory_space=pl.ANY)


def dft_tables():
    k8 = np.arange(8)
    turn = 2.0 * np.pi * np.outer(k8, k8) / 8.0
    c, s = np.cos(turn), np.sin(turn)
    eye = np.eye(4)
    inner = np.block([[np.kron(eye, c), np.kron(eye, s)], [-np.kron(eye, s), np.kron(eye, c)]])
    inner = np.concatenate([inner, inner], axis=1)
    m = np.arange(LANES) // SUB
    turn = 2.0 * np.pi * np.outer(k8, m) / 32.0
    twiddle = np.stack([np.cos(turn), -np.sin(turn)])
    b = np.arange(LANES) % SUB
    turn = 2.0 * np.pi * (np.outer(m, m) / 4.0 + np.outer(b, b) / 32.0)
    c, s = np.cos(turn) / 1024.0, np.sin(turn) / 1024.0
    outer = np.block([[c, -s], [s, c]]).astype(np.float32)
    high = outer.astype(jnp.bfloat16)
    low = (outer - high.astype(np.float32)).astype(jnp.bfloat16)
    return (
        jnp.asarray(inner.astype(jnp.bfloat16)),
        jnp.asarray(twiddle.astype(np.float32)),
        jnp.asarray(np.stack([high, low])),
    )


def pack_kernel(cap, owner, base, tick, row, col, steps, vis, out, scr, count):
    peers, rows, _ = out.shape
    items = vis.shape[0]
    scr[...] = jnp.zeros_like(scr)
    for t in range(peers):
        count[t] = 0
    lane = lax.broadcasted_iota(jnp.int32, (1, LANES), 1)
    for i in range(items):
        o = owner[i]
        r = count[o]
        count[o] = r + 1
        at = pl.multiple_of(o * rows + r * 8, 8)
        scr[pl.ds(at, 8), :] = vis[i].astype(F32)
        b = base[i]
        c = col[i]
        values = (b // 256, b % 256, tick[i], row[i], c // 8, c % 8, steps[i])
        meta = jnp.zeros((1, LANES), jnp.int32)
        for f, value in enumerate(values):
            meta = jnp.where(lane == f, value, meta)
        scr[pl.ds(o * rows + cap * 8 + r, 1), :] = meta.astype(F32)
    for t in range(peers):
        out[t] = scr[t * rows : (t + 1) * rows, :].astype(BF16)


def cos_sin_turns(x):
    x = x - jnp.round(x)
    quarter = jnp.round(x * 4.0)
    y = (x - quarter * 0.25) * (2.0 * math.pi)
    z = y * y
    s = y * (1.0 + z * (-1.0 / 6 + z * (1.0 / 120 + z * (-1.0 / 5040 + z * (1.0 / 362880)))))
    c = 1.0 + z * (-0.5 + z * (1.0 / 24 + z * (-1.0 / 720 + z * (1.0 / 40320 + z * (-1.0 / 3628800)))))
    odd = jnp.abs(quarter) == 1.0
    negative_c = (quarter == 1.0) | (jnp.abs(quarter) == 2.0)
    negative_s = (quarter == -1.0) | (jnp.abs(quarter) == 2.0)
    cos = jnp.where(odd, s, c)
    sin = jnp.where(odd, c, s)
    return jnp.where(negative_c, -cos, cos), jnp.where(negative_s, -sin, sin)


def cmul(a, b):
    return a[0] * b[0] - a[1] * b[1], a[0] * b[1] + a[1] * b[0]


def conj(a):
    return a[0], -a[1]


def both(a, b):
    rr, ii, ri, ir = a[0] * b[0], a[1] * b[1], a[0] * b[1], a[1] * b[0]
    return (rr - ii, ri + ir), (rr + ii, ir - ri)


def split(x):
    high = x.astype(BF16)
    return high, (x - high.astype(F32)).astype(BF16)


def main_kernel(
    cap, recv, positions, freq, inner, twiddle, outer, screens,
    strip, up, down,
    meta, index, table, sky, screen, plane, acc, place, screen_sem, index_sem,
):
    peers, rows, _ = recv.shape
    slots = peers * cap
    groups = slots // 8
    stations = positions.shape[0]
    intervals = screens.shape[0] // stations
    tiles = strip.shape[2] // LANES
    lane = lax.broadcasted_iota(jnp.int32, (8, LANES), 1)
    step = (lane // (LANES // NT)).astype(F32)

    for t in range(peers):
        chunk = recv[t, cap * 8 : cap * 8 + 8, :].astype(F32)
        meta[t * cap : (t + 1) * cap, :] = chunk[:cap, :]

    m = meta[...]
    baseline = m[:, 0:1] * 256.0 + m[:, 1:2]
    tick = m[:, 2:3]
    series = lax.broadcasted_iota(jnp.int32, (1, stations), 1).astype(F32)
    offsets = series * (2.0 * stations - series - 1.0) * 0.5
    one = jnp.sum((offsets <= baseline).astype(F32), axis=1, keepdims=True) - 1.0
    two = baseline - one * (2.0 * stations - one - 1.0) * 0.5 + one + 1.0
    interval = jnp.floor(tick * (1.0 / BPER))
    column = m[:, 4:5] * 8.0 + m[:, 5:6]
    tile_a = jnp.floor(column * (1.0 / LANES))
    lane_a = column - tile_a * LANES
    tile_b = jnp.floor((column - LANES // 2) * (1.0 / LANES))
    lane_b = column - LANES // 2 - tile_b * LANES
    fits = lane_a <= LANES - SUB
    values = (
        one * intervals + interval,
        two * intervals + interval,
        m[:, 3:4],
        jnp.where(fits, tile_a, tile_b + tiles),
        jnp.where(fits, lane_a, lane_b),
    )
    wide = lax.broadcasted_iota(jnp.int32, (slots, LANES), 1)
    packed = jnp.zeros((slots, LANES), F32)
    for f, value in enumerate(values):
        packed = jnp.where(wide == f, value, packed)
    index[...] = packed.astype(jnp.int32)
    to_scalar = pltpu.make_async_copy(index, place, index_sem)
    to_scalar.start()

    station = lax.broadcasted_iota(jnp.int32, (1, stations), 1).astype(F32)
    chosen = (station == two).astype(F32) - (station == one).astype(F32)
    vector = jnp.dot(chosen, positions[...], precision=lax.Precision.HIGHEST, preferred_element_type=F32)
    meta[:, 8:11] = vector

    to_scalar.wait()

    def fetch(n, _):
        for side in range(2):
            entry = place[n, side]
            pltpu.make_async_copy(screens.at[entry], screen.at[n, side], screen_sem).start()
        return 0

    lax.fori_loop(0, slots, fetch, 0)

    channel = jnp.concatenate([freq[...], freq[...]], axis=1)

    def phases(g, _):
        here = meta[pl.ds(pl.multiple_of(g * 8, 8), 8), :]
        start = here[:, 2:3] * NT
        live = (step < here[:, 6:7]).astype(F32)
        x, y, z = here[:, 8:9], here[:, 9:10], here[:, 10:11]
        scale = hour_step / (2.0 * math.pi)
        cos_now, sin_now = cos_sin_turns(scale * (start + step))
        cos_mid, sin_mid = cos_sin_turns(scale * (start + 0.5 * (NT - 1) + 0.0 * step))

        def track(c, s):
            u = s * x + c * y
            v = (-math.sin(declination)) * c * x + math.sin(declination) * s * y + math.cos(declination) * z
            return u, v

        u_now, v_now = track(cos_now, sin_now)
        u_mid, v_mid = track(cos_mid, sin_mid)
        du = (u_now * channel - u_mid) * (1.0 / SUB)
        dv = (v_now * channel - v_mid) * (1.0 / SUB)
        e1 = cos_sin_turns(0.5 * du)
        e2 = cmul(e1, e1)
        e3 = cmul(e2, e1)
        e4 = cmul(e2, e2)
        e8 = cmul(e4, e4)
        g1 = cos_sin_turns(dv)
        g2 = cmul(g1, g1)
        g3 = cmul(g2, g1)
        g4 = cmul(g2, g2)
        g8 = cmul(g4, g4)
        g12 = cmul(g8, g4)
        mid = (e3[0] * live, e3[1] * live)
        ups = [mid]
        for _ in range(3):
            ups.append(cmul(ups[-1], e8))
        downs = [cmul(mid, conj(e8))]
        for _ in range(3):
            downs.append(cmul(downs[-1], conj(e8)))
        row_phase = downs[::-1] + ups
        ones = (jnp.ones_like(du), jnp.zeros_like(du))
        col_phase = [conj(g4), conj(g3), conj(g2), conj(g1), ones, g1, g2, g3]
        base = pl.multiple_of(g * (KINDS * 8), 8)

        def put(kind, value):
            table[pl.ds(base + kind * 8, 8), :] = value

        for k in range(8):
            put(k, row_phase[k][0])
            put(8 + k, row_phase[k][1])
            put(16 + k, col_phase[k][0])
            put(24 + k, col_phase[k][1])
        k = 32
        for e in (e1, e3):
            plus12, minus12 = both(e, g12)
            plus4, minus4 = both(e, g4)
            for value in (minus12, minus4, plus4, plus12):
                put(k, value[0])
                put(k + 8, value[1])
                k += 1
        return 0

    lax.fori_loop(0, groups, phases, 0)

    def image(n, _):
        g = n // 8
        base = g * (KINDS * 8) + n % 8

        def rows_of(kind):
            return table[pl.ds(base + kind * 8, 8, stride=8), :]

        def row_of(kind):
            return table[pl.ds(base + kind * 8, 1), :]

        row_phase = (rows_of(0), rows_of(8))
        col_phase = (rows_of(16), rows_of(24))
        cells = [[None] * 4 for _ in range(4)]
        for k in range(8):
            mi, bb = k // 4, k % 4
            plus, minus = both(col_phase, (row_of(32 + k), row_of(40 + k)))
            cells[2 + mi][bb] = plus
            cells[1 - mi][3 - bb] = minus
        real = jnp.concatenate([cells[a][b][0] for a in range(4) for b in range(4)], axis=0)
        imag = jnp.concatenate([cells[a][b][1] for a in range(4) for b in range(4)], axis=0)
        right = jnp.concatenate([real.astype(BF16), imag.astype(BF16)], axis=1)
        peer = n // cap
        block = recv[peer, pl.ds(pl.multiple_of((n % cap) * 8, 8), 8), :].astype(F32)
        reals, imags = [], []
        for p in range(4):
            value = cmul(row_phase, (block[2 * p : 2 * p + 1, :], block[2 * p + 1 : 2 * p + 2, :]))
            reals.append(value[0])
            imags.append(value[1])
        real = jnp.concatenate(reals, axis=0)
        imag = jnp.concatenate(imags, axis=0)
        left = jnp.concatenate(
            [jnp.concatenate([real, -imag], axis=1), jnp.concatenate([imag, real], axis=1)], axis=0
        )
        high, low = split(left)
        dims = (((1,), (1,)), ((), ()))
        out = lax.dot_general(jnp.concatenate([high, low], axis=0), right, dims, preferred_element_type=F32)
        sky[n] = out[:64] + out[64:]
        return 0

    lax.fori_loop(0, slots, image, 0, unroll=2)

    acc[...] = jnp.zeros_like(acc)

    def land(n, _):
        for side in range(2):
            pltpu.make_async_copy(screens.at[0], screen.at[n, side], screen_sem).wait()
        return 0

    lax.fori_loop(0, slots, land, 0)

    batch = plane.shape[0]

    def grid(g, _):
        results = []
        for u in range(batch):
            n = g * batch + u
            jones = []
            for side in range(2):
                data = screen[n, side].astype(F32)
                for j in range(8):
                    plane[u, side, j * 8 : (j + 1) * 8, :] = data[:, j * LANES : (j + 1) * LANES]
                entry = [plane[u, side, pl.ds(e, 8, stride=8), :] for e in range(8)]
                jones.append([(entry[2 * k], entry[2 * k + 1]) for k in range(4)])
            image = sky[n]
            value = [(image[8 * p : 8 * p + 8], image[32 + 8 * p : 40 + 8 * p]) for p in range(4)]
            left, right = jones

            def add(a, b):
                return a[0] + b[0], a[1] + b[1]

            mixed = [
                add(cmul(left[2 * i], value[k]), cmul(left[2 * i + 1], value[2 + k]))
                for i in range(2)
                for k in range(2)
            ]
            corrected = [
                add(cmul(mixed[2 * i], conj(right[2 * j])), cmul(mixed[2 * i + 1], conj(right[2 * j + 1])))
                for i in range(2)
                for j in range(2)
            ]
            stacked = jnp.concatenate([c[0] for c in corrected] + [c[1] for c in corrected], axis=0)
            high, low = split(stacked)
            turned = jnp.dot(inner[...], jnp.concatenate([high, low], axis=0), preferred_element_type=F32)
            tw = (twiddle[0], twiddle[1])
            spun = [cmul((turned[8 * p : 8 * p + 8], turned[32 + 8 * p : 40 + 8 * p]), tw) for p in range(4)]
            results.append(
                jnp.concatenate(
                    [jnp.concatenate([s[0] for s in spun], axis=0), jnp.concatenate([s[1] for s in spun], axis=0)],
                    axis=1,
                )
            )
        high, low = split(jnp.concatenate(results, axis=0))
        out = jnp.dot(high, outer[0], preferred_element_type=F32)
        out += jnp.dot(high, outer[1], preferred_element_type=F32)
        out += jnp.dot(low, outer[0], preferred_element_type=F32)
        for u in range(batch):
            n = g * batch + u
            first = place[n, 2]
            tile = place[n, 3]
            shift = place[n, 4]
            inside = (lane >= shift) & (lane < shift + SUB)
            for p in range(4):
                for r in range(2):
                    cell = out[u * 32 + 8 * p : u * 32 + 8 * p + 8, r * LANES : (r + 1) * LANES]
                    parts = []
                    for k4 in range(4):
                        turn = (shift + (LANES - SUB * k4)) % LANES
                        parts.append(jnp.where(inside, pltpu.roll(cell, turn, 1), 0.0))
                    spot = (tile, 2 * p + r, pl.ds(first, SUB), slice(None))
                    acc[spot] = acc[spot] + jnp.concatenate(parts, axis=0)
        return 0

    lax.fori_loop(0, slots // batch, grid, 0)

    half = lax.broadcasted_iota(jnp.int32, (STRIP + SUB, LANES), 1) < LANES // 2
    for plane_at in range(8):
        behind = None
        for t in range(tiles):
            value = acc[t, plane_at]
            turned = None
            if t < tiles - 1:
                turned = pltpu.roll(acc[tiles + t, plane_at], LANES // 2, 1)
                value = value + jnp.where(half, 0.0, turned)
            if behind is not None:
                value = value + jnp.where(half, behind, 0.0)
            behind = turned
            columns = slice(t * LANES, (t + 1) * LANES)
            up[plane_at, :, columns] = value[:HALF].astype(BF16)
            strip[plane_at, :, columns] = value[HALF : HALF + STRIP]
            down[plane_at, :, columns] = value[HALF + STRIP :].astype(BF16)


def add_kernel(strip, above, below, out):
    out[:, :HALF, :] = strip[:, :HALF, :] + above[...].astype(F32)
    out[:, HALF:, :] = strip[:, HALF:, :] + below[...].astype(F32)


def body(visibilities, screens, positions, channel_freq, owner, baseline, tick, row, col, steps):
    peers = lax.axis_size("tile")
    items = visibilities.shape[0]
    cap = max(2, 2 * items // peers)
    slots = peers * cap
    rows = cap * 8 + 8
    columns = 1024
    tiles = columns // LANES

    packed = pl.pallas_call(
        functools.partial(pack_kernel, cap),
        out_shape=jax.ShapeDtypeStruct((peers, rows, LANES), BF16),
        in_specs=[SMEM] * 6 + [VMEM],
        out_specs=VMEM,
        scratch_shapes=[pltpu.VMEM((peers * rows, LANES), F32), pltpu.SMEM((peers,), jnp.int32)],
        name="pack",
    )(owner[:, 0], baseline, tick, row, col, steps, visibilities)
    received = lax.all_to_all(packed, "tile", split_axis=0, concat_axis=0, tiled=True)

    inner, twiddle, outer = dft_tables()
    table = screens.reshape(screens.shape[0] * screens.shape[1], 8, SUB * SUB)
    batch = 4
    strip, up, down = pl.pallas_call(
        functools.partial(main_kernel, cap),
        out_shape=(
            jax.ShapeDtypeStruct((8, STRIP, columns), F32),
            jax.ShapeDtypeStruct((8, HALF, columns), BF16),
            jax.ShapeDtypeStruct((8, HALF, columns), BF16),
        ),
        in_specs=[VMEM] * 6 + [ANY],
        out_specs=(VMEM, VMEM, VMEM),
        scratch_shapes=[
            pltpu.VMEM((slots, LANES), F32),
            pltpu.VMEM((slots, LANES), jnp.int32),
            pltpu.VMEM((slots * KINDS, LANES), F32),
            pltpu.VMEM((slots, 64, LANES), F32),
            pltpu.VMEM((slots, 2, 8, SUB * SUB), BF16),
            pltpu.VMEM((batch, 2, 64, LANES), F32),
            pltpu.VMEM((2 * tiles - 1, 8, STRIP + SUB, LANES), F32),
            pltpu.SMEM((slots, LANES), jnp.int32),
            pltpu.SemaphoreType.DMA,
            pltpu.SemaphoreType.DMA,
        ],
        compiler_params=pltpu.CompilerParams(vmem_limit_bytes=40 * 1024 * 1024),
        name="grid_items",
    )(received, positions, channel_freq[None, :], inner, twiddle, outer, table)

    ends = peers - 1
    above = lax.ppermute(down, "tile", [(i, i + 1) for i in range(ends)])
    below = lax.ppermute(up, "tile", [(i + 1, i) for i in range(ends)])
    return pl.pallas_call(
        add_kernel,
        out_shape=jax.ShapeDtypeStruct(strip.shape, F32),
        in_specs=[VMEM] * 3,
        out_specs=VMEM,
        name="add_spill",
    )(strip, above, below)


def solution(mesh):
    return jax.shard_map(
        body,
        mesh=mesh,
        in_specs=(
            P(("band", "tile"), None, None),
            P("band", None, None, None),
            P(),
            P("band"),
            P(("band", "tile"), None),
            P(("band", "tile")),
            P(("band", "tile")),
            P(("band", "tile")),
            P(("band", "tile")),
            P(("band", "tile")),
        ),
        out_specs=P("band", "tile", None),
        check_vma=False,
    )
```

```python
import functools
import math

import jax
import jax.numpy as jnp
import numpy as np
from jax import lax
from jax.experimental import pallas as pl
from jax.experimental.pallas import tpu as pltpu
from jax.sharding import PartitionSpec as P

SUB = 32
NT = 2
BPER = 8
STRIP = 32
HALF = 16
GCOLS = 1024
LANES = 128
KINDS = 48

hour_step = 0.003
declination = -0.5

F32 = jnp.float32
BF16 = jnp.bfloat16
VMEM = pl.BlockSpec(memory_space=pltpu.VMEM)
SMEM = pl.BlockSpec(memory_space=pltpu.SMEM)
ANY = pl.BlockSpec(memory_space=pl.ANY)


def dft_tables():
    k8 = np.arange(8)
    turn = 2.0 * np.pi * np.outer(k8, k8) / 8.0
    c, s = np.cos(turn), np.sin(turn)
    eye = np.eye(4)
    inner = np.block([[np.kron(eye, c), np.kron(eye, s)], [-np.kron(eye, s), np.kron(eye, c)]])
    inner = np.concatenate([inner, inner], axis=1)
    m = np.arange(LANES) // SUB
    turn = 2.0 * np.pi * np.outer(k8, m) / 32.0
    twiddle = np.stack([np.cos(turn), -np.sin(turn)])
    b = np.arange(LANES) % SUB
    turn = 2.0 * np.pi * (np.outer(m, m) / 4.0 + np.outer(b, b) / 32.0)
    c, s = np.cos(turn) / 1024.0, np.sin(turn) / 1024.0
    outer = np.block([[c, -s], [s, c]]).astype(np.float32)
    high = outer.astype(jnp.bfloat16)
    low = (outer - high.astype(np.float32)).astype(jnp.bfloat16)
    return (
        jnp.asarray(inner.astype(jnp.bfloat16)),
        jnp.asarray(twiddle.astype(np.float32)),
        jnp.asarray(np.stack([high, low])),
    )


def pack_kernel(slots, owner, base, tick, row, col, steps, vis, out, scr, count):
    peers, rows, _ = out.shape
    items = vis.shape[0]
    scr[...] = jnp.zeros_like(scr)
    for t in range(peers + 1):
        count[t] = 0
    lane = lax.broadcasted_iota(jnp.int32, (1, LANES), 1)
    field = lane % (LANES // 2)
    for i in range(items):
        o = owner[i]
        w = row[i]
        b = base[i]
        c = col[i]
        values = (b // 256, b % 256, tick[i], 0, c // 8, c % 8, steps[i])
        common = jnp.zeros((1, LANES), jnp.int32)
        for f, value in enumerate(values):
            common = jnp.where(field == f, value, common)
        data = vis[i].astype(F32)
        near = jnp.where(w < HALF, o - 1, o + 1)
        spills = (w != HALF) & (near >= 0) & (near < peers)
        near = jnp.where(spills, near, peers)
        for target, start in ((o, w + HALF), (near, jnp.where(w < HALF, w + 48, w - HALF))):
            r = count[target]
            count[target] = jnp.where(target == peers, 0, r + 1)
            scr[pl.ds(pl.multiple_of(target * rows + r * 8, 8), 8), :] = data
            mine = (lane // (LANES // 2)) == r // 8
            at = pl.ds(target * rows + slots * 8 + r % 8, 1)
            record = jnp.where(field == 3, start, common).astype(F32)
            scr[at, :] = jnp.where(mine, record, scr[at, :])
    for t in range(peers):
        out[t] = scr[t * rows : (t + 1) * rows, :].astype(BF16)


def planes_kernel(screens, out, buffer, turned, sems):
    total = screens.shape[0]
    size = buffer.shape[1]
    parts = total // size

    def copy(part, slot):
        return pltpu.make_async_copy(screens.at[pl.ds(part * size, size)], buffer.at[slot], sems.at[slot])

    copy(0, 0).start()
    for part in range(parts):
        slot = part % 2
        if part + 1 < parts:
            copy(part + 1, 1 - slot).start()
        copy(part, slot).wait()

        def one(k, _):
            data = buffer[slot, k].astype(F32)
            for j in range(8):
                turned[k % 2, pl.ds(j, 8, stride=8), :] = data[:, j * LANES : (j + 1) * LANES]
            out[part * size + k] = turned[k % 2].astype(BF16)
            return 0

        lax.fori_loop(0, size, one, 0, unroll=2)


def cos_sin_turns(x):
    x = x - jnp.round(x)
    quarter = jnp.round(x * 4.0)
    y = (x - quarter * 0.25) * (2.0 * math.pi)
    z = y * y
    s = y * (1.0 + z * (-1.0 / 6 + z * (1.0 / 120 + z * (-1.0 / 5040 + z * (1.0 / 362880)))))
    c = 1.0 + z * (-0.5 + z * (1.0 / 24 + z * (-1.0 / 720 + z * (1.0 / 40320 + z * (-1.0 / 3628800)))))
    odd = jnp.abs(quarter) == 1.0
    negative_c = (quarter == 1.0) | (jnp.abs(quarter) == 2.0)
    negative_s = (quarter == -1.0) | (jnp.abs(quarter) == 2.0)
    cos = jnp.where(odd, s, c)
    sin = jnp.where(odd, c, s)
    return jnp.where(negative_c, -cos, cos), jnp.where(negative_s, -sin, sin)


def cmul(a, b):
    return a[0] * b[0] - a[1] * b[1], a[0] * b[1] + a[1] * b[0]


def conj(a):
    return a[0], -a[1]


def both(a, b):
    rr, ii, ri, ir = a[0] * b[0], a[1] * b[1], a[0] * b[1], a[1] * b[0]
    return (rr - ii, ri + ir), (rr + ii, ir - ri)


def split(x):
    high = x.astype(BF16)
    return high, (x - high.astype(F32)).astype(BF16)


def main_kernel(
    slots, recv, positions, freq, inner, twiddle, outer, planes,
    strip,
    meta, index, table, sky, screen, acc, place, index_sem, screen_sem,
):
    peers, rows, _ = recv.shape
    most = meta.shape[0]
    stations = positions.shape[0]
    intervals = planes.shape[0] // stations
    tiles = strip.shape[2] // LANES
    lane = lax.broadcasted_iota(jnp.int32, (8, LANES), 1)
    step = (lane // (LANES // NT)).astype(F32)

    halves = -(-slots // 8)
    sublane = lax.broadcasted_iota(jnp.int32, (8, LANES), 0)
    records = []
    for t in range(peers):
        chunk = recv[t, slots * 8 : slots * 8 + 8, :].astype(F32)
        for h in range(halves):
            record = pltpu.roll(chunk, LANES // 2, 1) if h else chunk
            record = jnp.where(lane == 7, float(t), record)
            records.append(jnp.where(lane == 8, (sublane + 8 * h).astype(F32), record))
    records = jnp.concatenate(records, axis=0)
    many = records.shape[0]
    filled = (records[:, 6:7] > 0.0).astype(F32)
    flags = jnp.where(lax.broadcasted_iota(jnp.int32, (many, LANES), 1) == 0, filled, 0.0).astype(BF16)
    dims = (((1,), (1,)), ((), ()))
    used = lax.dot_general(jnp.ones((8, LANES), BF16), flags, dims, preferred_element_type=F32)
    before = lax.broadcasted_iota(jnp.int32, (many, many), 0) < lax.broadcasted_iota(jnp.int32, (many, many), 1)
    rank = jnp.dot(used.astype(BF16), before.astype(F32).astype(BF16), preferred_element_type=F32)
    order = lax.broadcasted_iota(jnp.int32, (most, many), 0).astype(F32)
    pick = jnp.where((rank[0:1] == order) & (used[0:1] > 0.5), 1.0, 0.0)
    m = jnp.dot(pick.astype(BF16), records.astype(BF16), preferred_element_type=F32)
    meta[...] = m
    number = jnp.sum(filled).astype(jnp.int32)
    groups = (number + 7) // 8

    baseline = m[:, 0:1] * 256.0 + m[:, 1:2]
    tick = m[:, 2:3]
    series = lax.broadcasted_iota(jnp.int32, (1, stations), 1).astype(F32)
    offsets = series * (2.0 * stations - series - 1.0) * 0.5
    one = jnp.sum((offsets <= baseline).astype(F32), axis=1, keepdims=True) - 1.0
    two = baseline - one * (2.0 * stations - one - 1.0) * 0.5 + one + 1.0
    interval = jnp.floor(tick * (1.0 / BPER))
    column = m[:, 4:5] * 8.0 + m[:, 5:6]
    tile_a = jnp.floor(column * (1.0 / LANES))
    lane_a = column - tile_a * LANES
    tile_b = jnp.floor((column - LANES // 2) * (1.0 / LANES))
    lane_b = column - LANES // 2 - tile_b * LANES
    fits = lane_a <= LANES - SUB
    spare = float(2 * tiles - 1)
    values = (
        one * intervals + interval,
        two * intervals + interval,
        m[:, 3:4],
        jnp.where(m[:, 6:7] > 0.0, jnp.where(fits, tile_a, tile_b + tiles), spare),
        jnp.where(fits, lane_a, lane_b),
        m[:, 7:8],
        m[:, 8:9],
    )
    wide = lax.broadcasted_iota(jnp.int32, (most, LANES), 1)
    packed = jnp.zeros((most, LANES), F32)
    for f, value in enumerate(values):
        packed = jnp.where(wide == f, value, packed)
    index[...] = packed.astype(jnp.int32)
    to_scalar = pltpu.make_async_copy(index, place, index_sem)
    to_scalar.start()

    chosen = (series == two).astype(F32) - (series == one).astype(F32)
    vector = jnp.dot(chosen, positions[...], precision=lax.Precision.HIGHEST, preferred_element_type=F32)
    meta[:, 16:19] = vector

    channel = jnp.concatenate([freq[...], freq[...]], axis=1)

    def phases(g, _):
        here = meta[pl.ds(pl.multiple_of(g * 8, 8), 8), :]
        start = here[:, 2:3] * NT
        live = (step < here[:, 6:7]).astype(F32)
        x, y, z = here[:, 16:17], here[:, 17:18], here[:, 18:19]
        scale = hour_step / (2.0 * math.pi)
        cos_now, sin_now = cos_sin_turns(scale * (start + step))
        cos_mid, sin_mid = cos_sin_turns(scale * (start + 0.5 * (NT - 1) + 0.0 * step))

        def track(c, s):
            u = s * x + c * y
            v = (-math.sin(declination)) * c * x + math.sin(declination) * s * y + math.cos(declination) * z
            return u, v

        u_now, v_now = track(cos_now, sin_now)
        u_mid, v_mid = track(cos_mid, sin_mid)
        du = (u_now * channel - u_mid) * (1.0 / SUB)
        dv = (v_now * channel - v_mid) * (1.0 / SUB)
        e1 = cos_sin_turns(0.5 * du)
        e2 = cmul(e1, e1)
        e3 = cmul(e2, e1)
        e4 = cmul(e2, e2)
        e8 = cmul(e4, e4)
        g1 = cos_sin_turns(dv)
        g2 = cmul(g1, g1)
        g3 = cmul(g2, g1)
        g4 = cmul(g2, g2)
        g8 = cmul(g4, g4)
        g12 = cmul(g8, g4)
        mid = (e3[0] * live, e3[1] * live)
        ups = [mid]
        for _ in range(3):
            ups.append(cmul(ups[-1], e8))
        downs = [cmul(mid, conj(e8))]
        for _ in range(3):
            downs.append(cmul(downs[-1], conj(e8)))
        row_phase = downs[::-1] + ups
        ones = (jnp.ones_like(du), jnp.zeros_like(du))
        col_phase = [conj(g4), conj(g3), conj(g2), conj(g1), ones, g1, g2, g3]
        base = pl.multiple_of(g * (KINDS * 8), 8)

        def put(kind, value):
            table[pl.ds(base + kind * 8, 8), :] = value

        for k in range(8):
            put(k, row_phase[k][0])
            put(8 + k, row_phase[k][1])
            put(16 + k, col_phase[k][0])
            put(24 + k, col_phase[k][1])
        k = 32
        for e in (e1, e3):
            plus12, minus12 = both(e, g12)
            plus4, minus4 = both(e, g4)
            for value in (minus12, minus4, plus4, plus12):
                put(k, value[0])
                put(k + 8, value[1])
                k += 1
        return 0

    lax.fori_loop(0, groups, phases, 0)
    to_scalar.wait()

    def image(g, u):
        n = g * 8 + u
        base = g * (KINDS * 8) + u

        def rows_of(kind):
            return table[pl.ds(base + kind * 8, 8, stride=8), :]

        def row_of(kind):
            return table[pl.ds(base + kind * 8, 1), :]

        row_phase = (rows_of(0), rows_of(8))
        col_phase = (rows_of(16), rows_of(24))
        cells = [[None] * 4 for _ in range(4)]
        for k in range(8):
            mi, bb = k // 4, k % 4
            plus, minus = both(col_phase, (row_of(32 + k), row_of(40 + k)))
            cells[2 + mi][bb] = plus
            cells[1 - mi][3 - bb] = minus
        real = jnp.concatenate([cells[a][b][0] for a in range(4) for b in range(4)], axis=0)
        imag = jnp.concatenate([cells[a][b][1] for a in range(4) for b in range(4)], axis=0)
        right = jnp.concatenate([real.astype(BF16), imag.astype(BF16)], axis=1)
        block = recv[place[n, 5], pl.ds(pl.multiple_of(place[n, 6] * 8, 8), 8), :].astype(F32)
        reals, imags = [], []
        for p in range(4):
            value = cmul(row_phase, (block[2 * p : 2 * p + 1, :], block[2 * p + 1 : 2 * p + 2, :]))
            reals.append(value[0])
            imags.append(value[1])
        real = jnp.concatenate(reals, axis=0)
        imag = jnp.concatenate(imags, axis=0)
        left = jnp.concatenate(
            [jnp.concatenate([real, -imag], axis=1), jnp.concatenate([imag, real], axis=1)], axis=0
        )
        high, low = split(left)
        out = lax.dot_general(jnp.concatenate([high, low], axis=0), right, dims, preferred_element_type=F32)
        sky[n] = out[:64] + out[64:]

    def images(g, _):
        for u in range(8):
            for side in range(2):
                n = g * 8 + u
                copy = pltpu.make_async_copy(planes.at[place[n, side]], screen.at[2 * n + side], screen_sem)
                copy.start()
        for u in range(8):
            image(g, u)
        return 0

    lax.fori_loop(0, groups, images, 0)

    acc[:, :, STRIP : 2 * STRIP, :] = jnp.zeros((2 * tiles, 8, STRIP, LANES), F32)
    batch = 8

    def land(g, _):
        here = screen.at[pl.ds(g * 2 * batch, 2 * batch)]
        pltpu.make_async_copy(planes.at[pl.ds(0, 2 * batch)], here, screen_sem).wait()
        return 0

    lax.fori_loop(0, groups, land, 0)

    def grid(g, _):
        results = []
        for u in range(batch):
            n = g * batch + u
            jones = []
            for side in range(2):
                entry = [screen[2 * n + side, 16 * k : 16 * k + 16, :].astype(F32) for k in range(4)]
                jones.append([(e[:8], e[8:]) for e in entry])
            image = sky[n]
            value = [(image[8 * p : 8 * p + 8], image[32 + 8 * p : 40 + 8 * p]) for p in range(4)]
            left, right = jones

            def add(a, b):
                return a[0] + b[0], a[1] + b[1]

            mixed = [
                add(cmul(left[2 * i], value[k]), cmul(left[2 * i + 1], value[2 + k]))
                for i in range(2)
                for k in range(2)
            ]
            corrected = [
                add(cmul(mixed[2 * i], conj(right[2 * j])), cmul(mixed[2 * i + 1], conj(right[2 * j + 1])))
                for i in range(2)
                for j in range(2)
            ]
            stacked = jnp.concatenate([c[0] for c in corrected] + [c[1] for c in corrected], axis=0)
            high, low = split(stacked)
            turned = jnp.dot(inner[...], jnp.concatenate([high, low], axis=0), preferred_element_type=F32)
            tw = (twiddle[0], twiddle[1])
            spun = [cmul((turned[8 * p : 8 * p + 8], turned[32 + 8 * p : 40 + 8 * p]), tw) for p in range(4)]
            results.append(
                jnp.concatenate(
                    [jnp.concatenate([s[0] for s in spun], axis=0), jnp.concatenate([s[1] for s in spun], axis=0)],
                    axis=1,
                )
            )
        high, low = split(jnp.concatenate(results, axis=0))
        out = jnp.dot(high, outer[0], preferred_element_type=F32)
        out += jnp.dot(high, outer[1], preferred_element_type=F32)
        out += jnp.dot(low, outer[0], preferred_element_type=F32)
        for u in range(batch):
            n = g * batch + u
            first = place[n, 2]
            tile = place[n, 3]
            shift = place[n, 4]
            inside = (lane >= shift) & (lane < shift + SUB)
            for p in range(4):
                for r in range(2):
                    cell = out[u * 32 + 8 * p : u * 32 + 8 * p + 8, r * LANES : (r + 1) * LANES]
                    parts = []
                    for k4 in range(4):
                        turn = (shift + (LANES - SUB * k4)) % LANES
                        parts.append(jnp.where(inside, pltpu.roll(cell, turn, 1), 0.0))
                    spot = (tile, 2 * p + r, pl.ds(first, SUB), slice(None))
                    acc[spot] = acc[spot] + jnp.concatenate(parts, axis=0)
        return 0

    lax.fori_loop(0, groups, grid, 0)

    half = lax.broadcasted_iota(jnp.int32, (STRIP, LANES), 1) < LANES // 2
    mine = slice(STRIP, 2 * STRIP)
    for plane_at in range(8):
        behind = None
        for t in range(tiles):
            value = acc[t, plane_at, mine, :]
            turned = None
            if t < tiles - 1:
                turned = pltpu.roll(acc[tiles + t, plane_at, mine, :], LANES // 2, 1)
                value = value + jnp.where(half, 0.0, turned)
            if behind is not None:
                value = value + jnp.where(half, behind, 0.0)
            behind = turned
            strip[plane_at, :, t * LANES : (t + 1) * LANES] = value


def body(visibilities, screens, positions, channel_freq, owner, baseline, tick, row, col, steps):
    peers = lax.axis_size("tile")
    items = visibilities.shape[0]
    slots = 3 * max(2, 2 * items // peers)
    rows = slots * 8 + 8
    most = -(-peers * slots // 8) * 8
    columns = GCOLS
    tiles = columns // LANES

    packed = pl.pallas_call(
        functools.partial(pack_kernel, slots),
        out_shape=jax.ShapeDtypeStruct((peers, rows, LANES), BF16),
        in_specs=[SMEM] * 6 + [VMEM],
        out_specs=VMEM,
        scratch_shapes=[pltpu.VMEM(((peers + 1) * rows, LANES), F32), pltpu.SMEM((peers + 1,), jnp.int32)],
        name="pack",
    )(owner[:, 0], baseline, tick, row, col, steps, visibilities)
    received = lax.all_to_all(packed, "tile", split_axis=0, concat_axis=0, tiled=True)

    table = screens.reshape(screens.shape[0] * screens.shape[1], 8, SUB * SUB)
    total = table.shape[0]
    planes = pl.pallas_call(
        planes_kernel,
        out_shape=jax.ShapeDtypeStruct((total, 64, LANES), BF16),
        in_specs=[ANY],
        out_specs=VMEM,
        scratch_shapes=[pltpu.VMEM((2, screens.shape[0], 8, SUB * SUB), BF16), pltpu.VMEM((2, 64, LANES), F32), pltpu.SemaphoreType.DMA((2,))],
        cost_estimate=pl.CostEstimate(flops=10**8, bytes_accessed=3 * 10**7, transcendentals=0),
        compiler_params=pltpu.CompilerParams(vmem_limit_bytes=24 * 1024 * 1024),
        name="screen_planes",
    )(table)

    inner, twiddle, outer = dft_tables()
    return pl.pallas_call(
        functools.partial(main_kernel, slots),
        out_shape=jax.ShapeDtypeStruct((8, STRIP, columns), F32),
        in_specs=[VMEM] * 6 + [ANY],
        out_specs=VMEM,
        scratch_shapes=[
            pltpu.VMEM((most, LANES), F32),
            pltpu.VMEM((most, LANES), jnp.int32),
            pltpu.VMEM((most * KINDS, LANES), F32),
            pltpu.VMEM((most, 64, LANES), F32),
            pltpu.VMEM((2 * most, 64, LANES), BF16),
            pltpu.VMEM((2 * tiles, 8, 3 * STRIP, LANES), F32),
            pltpu.SMEM((most, LANES), jnp.int32),
            pltpu.SemaphoreType.DMA,
            pltpu.SemaphoreType.DMA,
        ],
        compiler_params=pltpu.CompilerParams(vmem_limit_bytes=56 * 1024 * 1024),
        name="grid_items",
    )(received, positions, channel_freq[None, :], inner, twiddle, outer, planes)


def solution(mesh):
    return jax.shard_map(
        body,
        mesh=mesh,
        in_specs=(
            P(("band", "tile"), None, None),
            P("band", None, None, None),
            P(),
            P("band"),
            P(("band", "tile"), None),
            P(("band", "tile")),
            P(("band", "tile")),
            P(("band", "tile")),
            P(("band", "tile")),
            P(("band", "tile")),
        ),
        out_specs=P("band", "tile", None),
        check_vma=False,
    )
```

```python
import functools
import math

import jax
import jax.numpy as jnp
import numpy as np
from jax import lax
from jax.experimental import pallas as pl
from jax.experimental.pallas import tpu as pltpu
from jax.sharding import PartitionSpec as P

SUB = 32
NT = 2
BPER = 8
STRIP = 32
HALF = 16
GCOLS = 1024
LANES = 128
KINDS = 48

hour_step = 0.003
declination = -0.5

F32 = jnp.float32
BF16 = jnp.bfloat16
VMEM = pl.BlockSpec(memory_space=pltpu.VMEM)
SMEM = pl.BlockSpec(memory_space=pltpu.SMEM)
ANY = pl.BlockSpec(memory_space=pl.ANY)


def dft_tables():
    k8 = np.arange(8)
    turn = 2.0 * np.pi * np.outer(k8, k8) / 8.0
    c, s = np.cos(turn), np.sin(turn)
    eye = np.eye(4)
    inner = np.block([[np.kron(eye, c), np.kron(eye, s)], [-np.kron(eye, s), np.kron(eye, c)]])
    inner = np.concatenate([inner, inner], axis=1)
    m = np.arange(LANES) // SUB
    turn = 2.0 * np.pi * np.outer(k8, m) / 32.0
    twiddle = np.stack([np.cos(turn), -np.sin(turn)])
    b = np.arange(LANES) % SUB
    turn = 2.0 * np.pi * (np.outer(m, m) / 4.0 + np.outer(b, b) / 32.0)
    c, s = np.cos(turn) / 1024.0, np.sin(turn) / 1024.0
    outer = np.block([[c, -s], [s, c]]).astype(np.float32)
    high = outer.astype(jnp.bfloat16)
    low = (outer - high.astype(np.float32)).astype(jnp.bfloat16)
    return (
        jnp.asarray(inner.astype(jnp.bfloat16)),
        jnp.asarray(twiddle.astype(np.float32)),
        jnp.asarray(np.stack([high, low])),
    )


def pack_kernel(
    slots, intervals, columns, owner, row, base, tick, col, steps, positions, vis, out, scr, notes, record, count
):
    peers, rows, _ = out.shape
    items = vis.shape[0]
    stations = positions.shape[1]
    tiles = columns // LANES
    dims = (((1,), (1,)), ((), ()))
    best = lax.Precision.HIGHEST
    scr[...] = jnp.zeros_like(scr)
    notes[...] = jnp.zeros_like(notes)
    for t in range(peers + 1):
        count[t] = 0

    lines = jnp.concatenate([base[...], tick[...], col[...], steps[...]], axis=0).astype(F32)
    unit = lax.broadcasted_iota(jnp.int32, (items, items), 0) == lax.broadcasted_iota(jnp.int32, (items, items), 1)
    m = lax.dot_general(unit.astype(F32), lines, dims, precision=best, preferred_element_type=F32)
    m = jnp.round(m)
    baseline, time, column, valid = m[:, 0:1], m[:, 1:2], m[:, 2:3], m[:, 3:4]
    series = lax.broadcasted_iota(jnp.int32, (1, stations), 1).astype(F32)
    offsets = series * (2.0 * stations - series - 1.0) * 0.5
    one = jnp.sum((offsets <= baseline).astype(F32), axis=1, keepdims=True) - 1.0
    two = baseline - one * (2.0 * stations - one - 1.0) * 0.5 + one + 1.0
    chosen = (series == two).astype(F32) - (series == one).astype(F32)
    vector = lax.dot_general(chosen, positions[...], dims, precision=best, preferred_element_type=F32)
    high, rest = split(vector)
    rest = vector - high.astype(F32)
    middle, low = split(rest)
    tile_a = jnp.floor(column * (1.0 / LANES))
    lane_a = column - tile_a * LANES
    tile_b = jnp.floor((column - LANES // 2) * (1.0 / LANES))
    lane_b = column - LANES // 2 - tile_b * LANES
    fits = lane_a <= LANES - SUB
    values = {
        0: one,
        1: two,
        2: time,
        4: jnp.where(fits, tile_a, tile_b + tiles) + 1.0,
        5: jnp.where(fits, lane_a, lane_b),
        6: valid,
        9: jnp.floor(time * (1.0 / BPER)),
    }
    for axis in range(3):
        for k, part in enumerate((high.astype(F32), middle.astype(F32), low.astype(F32))):
            values[16 + 3 * axis + k] = part[:, axis : axis + 1]
    field = lax.broadcasted_iota(jnp.int32, (items, LANES), 1) % (LANES // 2)
    total = jnp.zeros((items, LANES), F32)
    for f, value in values.items():
        total = jnp.where(field == f, value, total)
    record[...] = total

    lane = lax.broadcasted_iota(jnp.int32, (1, LANES), 1)
    third = lane % (LANES // 2) == 3
    for i in range(items):
        o = owner[i]
        w = row[i]
        data = vis[i].astype(F32)
        common = record[i : i + 1, :]
        above = w < HALF
        near = jnp.where(above, o - 1, o + 1)
        spills = (w != HALF) & (near >= 0) & (near < peers)
        near = jnp.where(spills, near, peers)
        for target, start in ((o, w + HALF), (near, jnp.where(above, w + 48, w - HALF))):
            r = count[target]
            count[target] = jnp.where(target == peers, 0, r + 1)
            scr[pl.ds(pl.multiple_of(target * rows + r * 8, 8), 8), :] = data
            notes[pl.ds(target * 16 + r, 1), :] = jnp.where(third, start.astype(F32), common)
    lower = lax.broadcasted_iota(jnp.int32, (8, LANES), 1) < LANES // 2
    for t in range(peers):
        out[t, : slots * 8, :] = scr[t * rows : t * rows + slots * 8, :].astype(BF16)
        note = jnp.where(lower, notes[t * 16 : t * 16 + 8, :], notes[t * 16 + 8 : t * 16 + 16, :])
        out[t, slots * 8 :, :] = note.astype(BF16)


def planes_kernel(screens, out, buffer, turned, result, sems, out_sems):
    total = screens.shape[0]
    size = buffer.shape[1]
    parts = -(-total // size)
    starts = [min(part * size, total - size) for part in range(parts)]

    def load(part):
        slot = part % 3
        return pltpu.make_async_copy(screens.at[pl.ds(starts[part], size)], buffer.at[slot], sems.at[slot])

    def save(part):
        slot = part % 2
        return pltpu.make_async_copy(result.at[slot], out.at[pl.ds(starts[part], size)], out_sems.at[slot])

    load(0).start()
    if parts > 1:
        load(1).start()
    for part in range(parts):
        load(part).wait()
        if part + 2 < parts:
            load(part + 2).start()
        if part > 1:
            save(part - 2).wait()

        def some(h, _):
            for u in range(4):
                k = h * 4 + u
                data = buffer[part % 3, k].astype(F32)
                for j in range(8):
                    turned[u, pl.ds(j, 8, stride=8), :] = data[:, j * LANES : (j + 1) * LANES]
            for u in range(4):
                result[part % 2, h * 4 + u] = turned[u].astype(BF16)
            return 0

        lax.fori_loop(0, size // 4, some, 0)
        if part > 0 and starts[part] < starts[part - 1] + size:
            save(part - 1).wait()
            save(part).start()
            save(part).wait()
        else:
            save(part).start()
    overlap = parts > 1 and starts[-1] < starts[-2] + size
    if not overlap:
        if parts > 1:
            save(parts - 2).wait()
        save(parts - 1).wait()


def cos_sin_turns(x):
    x = x - jnp.round(x)
    quarter = jnp.round(x * 4.0)
    y = (x - quarter * 0.25) * (2.0 * math.pi)
    z = y * y
    s = y * (1.0 + z * (-1.0 / 6 + z * (1.0 / 120 + z * (-1.0 / 5040 + z * (1.0 / 362880)))))
    c = 1.0 + z * (-0.5 + z * (1.0 / 24 + z * (-1.0 / 720 + z * (1.0 / 40320 + z * (-1.0 / 3628800)))))
    odd = jnp.abs(quarter) == 1.0
    negative_c = (quarter == 1.0) | (jnp.abs(quarter) == 2.0)
    negative_s = (quarter == -1.0) | (jnp.abs(quarter) == 2.0)
    cos = jnp.where(odd, s, c)
    sin = jnp.where(odd, c, s)
    return jnp.where(negative_c, -cos, cos), jnp.where(negative_s, -sin, sin)


def cmul(a, b):
    return a[0] * b[0] - a[1] * b[1], a[0] * b[1] + a[1] * b[0]


def conj(a):
    return a[0], -a[1]


def both(a, b):
    rr, ii, ri, ir = a[0] * b[0], a[1] * b[1], a[0] * b[1], a[1] * b[0]
    return (rr - ii, ri + ir), (rr + ii, ir - ri)


def split(x):
    high = x.astype(BF16)
    return high, (x - high.astype(F32)).astype(BF16)


def main_kernel(
    slots, intervals, recv, freq_hbm, inner_hbm, twiddle_hbm, outer_hbm, planes,
    strip,
    meta, index, table, sky, screen, acc, place, freq, inner, twiddle, outer,
    index_sem, screen_sems, table_sems,
):
    peers, rows, _ = recv.shape
    most = meta.shape[0]
    tiles = strip.shape[2] // LANES
    lane = lax.broadcasted_iota(jnp.int32, (8, LANES), 1)
    step = (lane // (LANES // NT)).astype(F32)

    tables = [
        pltpu.make_async_copy(source, target, table_sems.at[k])
        for k, (source, target) in enumerate(
            ((freq_hbm, freq), (inner_hbm, inner), (twiddle_hbm, twiddle), (outer_hbm, outer))
        )
    ]
    for copy in tables:
        copy.start()

    halves = -(-slots // 8)
    sublane = lax.broadcasted_iota(jnp.int32, (8, LANES), 0)
    records = []
    for t in range(peers):
        chunk = recv[t, slots * 8 : slots * 8 + 8, :].astype(F32)
        for h in range(halves):
            record = pltpu.roll(chunk, LANES // 2, 1) if h else chunk
            record = jnp.where(lane == 7, float(t), record)
            records.append(jnp.where(lane == 8, (sublane + 8 * h).astype(F32), record))
    records = jnp.concatenate(records, axis=0)
    many = records.shape[0]
    filled = (records[:, 6:7] > 0.0).astype(F32)
    flags = jnp.where(lax.broadcasted_iota(jnp.int32, (many, LANES), 1) == 0, filled, 0.0).astype(BF16)
    dims = (((1,), (1,)), ((), ()))
    used = lax.dot_general(jnp.ones((8, LANES), BF16), flags, dims, preferred_element_type=F32)
    before = lax.broadcasted_iota(jnp.int32, (many, many), 0) < lax.broadcasted_iota(jnp.int32, (many, many), 1)
    rank = jnp.dot(used.astype(BF16), before.astype(F32).astype(BF16), preferred_element_type=F32)
    order = lax.broadcasted_iota(jnp.int32, (most, many), 0).astype(F32)
    pick = jnp.where((rank[0:1] == order) & (used[0:1] > 0.5), 1.0, 0.0)
    m = jnp.dot(pick.astype(BF16), records.astype(BF16), preferred_element_type=F32)
    meta[...] = m
    number = jnp.sum(filled).astype(jnp.int32)
    groups = (number + 7) // 8

    field = lax.broadcasted_iota(jnp.int32, (8, LANES), 0)
    pickers = jnp.zeros((8, LANES), F32)
    for f, source in enumerate((0, 1, 3, 4, 5, 7, 8, 9)):
        pickers = jnp.where((field == f) & (lane == source), 1.0, pickers)
    width = index.shape[1]
    wide = m.astype(BF16)
    if width > most:
        wide = jnp.concatenate([wide, jnp.zeros((width - most, LANES), BF16)], axis=0)
    fields = lax.dot_general(pickers.astype(BF16), wide, dims, preferred_element_type=F32)
    index[...] = fields.astype(jnp.int32)
    to_scalar = pltpu.make_async_copy(index, place, index_sem)
    to_scalar.start()

    tables[0].wait()

    channel = jnp.concatenate([freq[...], freq[...]], axis=1)

    def phases(g, _):
        here = meta[pl.ds(pl.multiple_of(g * 8, 8), 8), :]
        start = here[:, 2:3] * NT
        live = (step < here[:, 6:7]).astype(F32)
        x, y, z = [sum(here[:, 16 + 3 * a + k : 17 + 3 * a + k] for k in range(3)) for a in range(3)]
        scale = hour_step / (2.0 * math.pi)
        cos_now, sin_now = cos_sin_turns(scale * (start + step))
        cos_mid, sin_mid = cos_sin_turns(scale * (start + 0.5 * (NT - 1) + 0.0 * step))

        def track(c, s):
            u = s * x + c * y
            v = (-math.sin(declination)) * c * x + math.sin(declination) * s * y + math.cos(declination) * z
            return u, v

        u_now, v_now = track(cos_now, sin_now)
        u_mid, v_mid = track(cos_mid, sin_mid)
        du = (u_now * channel - u_mid) * (1.0 / SUB)
        dv = (v_now * channel - v_mid) * (1.0 / SUB)
        e1 = cos_sin_turns(0.5 * du)
        e2 = cmul(e1, e1)
        e3 = cmul(e2, e1)
        e4 = cmul(e2, e2)
        e8 = cmul(e4, e4)
        g1 = cos_sin_turns(dv)
        g2 = cmul(g1, g1)
        g3 = cmul(g2, g1)
        g4 = cmul(g2, g2)
        g8 = cmul(g4, g4)
        g12 = cmul(g8, g4)
        mid = (e3[0] * live, e3[1] * live)
        ups = [mid]
        for _ in range(3):
            ups.append(cmul(ups[-1], e8))
        downs = [cmul(mid, conj(e8))]
        for _ in range(3):
            downs.append(cmul(downs[-1], conj(e8)))
        row_phase = downs[::-1] + ups
        ones = (jnp.ones_like(du), jnp.zeros_like(du))
        col_phase = [conj(g4), conj(g3), conj(g2), conj(g1), ones, g1, g2, g3]
        base = pl.multiple_of(g * (KINDS * 8), 8)

        def put(kind, value):
            table[pl.ds(base + kind * 8, 8), :] = value

        for k in range(8):
            put(k, row_phase[k][0])
            put(8 + k, row_phase[k][1])
            put(16 + k, col_phase[k][0])
            put(24 + k, col_phase[k][1])
        k = 32
        for e in (e1, e3):
            plus12, minus12 = both(e, g12)
            plus4, minus4 = both(e, g4)
            for value in (minus12, minus4, plus4, plus12):
                put(k, value[0])
                put(k + 8, value[1])
                k += 1
        return 0

    lax.fori_loop(0, groups, phases, 0)
    to_scalar.wait()

    def image(g, u):
        n = g * 8 + u
        base = g * (KINDS * 8) + u

        def rows_of(kind):
            return table[pl.ds(base + kind * 8, 8, stride=8), :]

        def row_of(kind):
            return table[pl.ds(base + kind * 8, 1), :]

        row_phase = (rows_of(0), rows_of(8))
        col_phase = (rows_of(16), rows_of(24))
        cells = [[None] * 4 for _ in range(4)]
        for k in range(8):
            mi, bb = k // 4, k % 4
            plus, minus = both(col_phase, (row_of(32 + k), row_of(40 + k)))
            cells[2 + mi][bb] = plus
            cells[1 - mi][3 - bb] = minus
        real = jnp.concatenate([cells[a][b][0] for a in range(4) for b in range(4)], axis=0)
        imag = jnp.concatenate([cells[a][b][1] for a in range(4) for b in range(4)], axis=0)
        right = jnp.concatenate([real.astype(BF16), imag.astype(BF16)], axis=1)
        block = recv[place[5, n], pl.ds(pl.multiple_of(place[6, n] * 8, 8), 8), :].astype(F32)
        reals, imags = [], []
        for p in range(4):
            value = cmul(row_phase, (block[2 * p : 2 * p + 1, :], block[2 * p + 1 : 2 * p + 2, :]))
            reals.append(value[0])
            imags.append(value[1])
        real = jnp.concatenate(reals, axis=0)
        imag = jnp.concatenate(imags, axis=0)
        left = jnp.concatenate(
            [jnp.concatenate([real, -imag], axis=1), jnp.concatenate([imag, real], axis=1)], axis=0
        )
        sky[n] = lax.dot_general(left.astype(BF16), right, dims, preferred_element_type=F32)

    batch = 8
    last = most // batch - 1

    def images(g):
        for u in range(batch):
            image(g, u)

    def fetch(g, way):
        for u in range(batch):
            for side in range(2):
                n = g * batch + u
                source = planes.at[place[side, n] * intervals + place[7, n]]
                pltpu.make_async_copy(source, screen.at[2 * n + side], screen_sems.at[way]).start()

    def land(g, way):
        here = screen.at[pl.ds(g * 2 * batch, 2 * batch)]
        pltpu.make_async_copy(planes.at[pl.ds(0, 2 * batch)], here, screen_sems.at[way]).wait()

    fetch(0, 0)
    images(0)
    for copy in tables[1:]:
        copy.wait()
    acc[:, :, STRIP : 2 * STRIP, :] = jnp.zeros((2 * tiles, 8, STRIP, LANES), F32)

    def grid(g, _):
        after = jnp.minimum(g + 1, last)
        land(g, g % 2)
        fetch(after, 1 - g % 2)
        results = []
        for u in range(batch):
            n = g * batch + u
            jones = []
            for side in range(2):
                entry = [screen[2 * n + side, 16 * k : 16 * k + 16, :].astype(F32) for k in range(4)]
                jones.append([(e[:8], e[8:]) for e in entry])
            image = sky[n]
            value = [(image[8 * p : 8 * p + 8], image[32 + 8 * p : 40 + 8 * p]) for p in range(4)]
            left, right = jones

            def add(a, b):
                return a[0] + b[0], a[1] + b[1]

            mixed = [
                add(cmul(left[2 * i], value[k]), cmul(left[2 * i + 1], value[2 + k]))
                for i in range(2)
                for k in range(2)
            ]
            corrected = [
                add(cmul(mixed[2 * i], conj(right[2 * j])), cmul(mixed[2 * i + 1], conj(right[2 * j + 1])))
                for i in range(2)
                for j in range(2)
            ]
            stacked = jnp.concatenate([c[0] for c in corrected] + [c[1] for c in corrected], axis=0)
            high, low = split(stacked)
            turned = jnp.dot(inner[...], jnp.concatenate([high, low], axis=0), preferred_element_type=F32)
            tw = (twiddle[0], twiddle[1])
            spun = [cmul((turned[8 * p : 8 * p + 8], turned[32 + 8 * p : 40 + 8 * p]), tw) for p in range(4)]
            results.append(
                jnp.concatenate(
                    [jnp.concatenate([s[0] for s in spun], axis=0), jnp.concatenate([s[1] for s in spun], axis=0)],
                    axis=1,
                )
            )
        high, low = split(jnp.concatenate(results, axis=0))
        out = jnp.dot(high, outer[0], preferred_element_type=F32)
        out += jnp.dot(high, outer[1], preferred_element_type=F32)
        out += jnp.dot(low, outer[0], preferred_element_type=F32)
        images(after)
        for u in range(batch):
            n = g * batch + u
            first = place[2, n]
            tile = place[3, n]
            shift = place[4, n]
            inside = (lane >= shift) & (lane < shift + SUB)
            cells = []
            for p in range(4):
                for r in range(2):
                    cell = out[u * 32 + 8 * p : u * 32 + 8 * p + 8, r * LANES : (r + 1) * LANES]
                    parts = []
                    for k4 in range(4):
                        turn = (shift + (LANES - SUB * k4)) % LANES
                        parts.append(jnp.where(inside, pltpu.roll(cell, turn, 1), 0.0))
                    cells.append(jnp.concatenate(parts, axis=0))
            spot = (tile, slice(None), pl.ds(first, SUB), slice(None))
            acc[spot] = acc[spot] + jnp.stack(cells)
        return 0

    lax.fori_loop(0, groups, grid, 0)
    land(jnp.minimum(groups, last), groups % 2)

    half = lax.broadcasted_iota(jnp.int32, (STRIP, LANES), 1) < LANES // 2
    mine = slice(STRIP, 2 * STRIP)
    for plane_at in range(8):
        behind = None
        for t in range(tiles):
            value = acc[1 + t, plane_at, mine, :]
            turned = None
            if t < tiles - 1:
                turned = pltpu.roll(acc[1 + tiles + t, plane_at, mine, :], LANES // 2, 1)
                value = value + jnp.where(half, 0.0, turned)
            if behind is not None:
                value = value + jnp.where(half, behind, 0.0)
            behind = turned
            strip[plane_at, :, t * LANES : (t + 1) * LANES] = value


def body(visibilities, screens, positions, channel_freq, owner, baseline, tick, row, col, steps):
    peers = lax.axis_size("tile")
    items = visibilities.shape[0]
    slots = 3 * max(2, 2 * items // peers)
    rows = slots * 8 + 8
    most = -(-peers * slots // 8) * 8
    wide = -(-most // LANES) * LANES
    columns = GCOLS
    tiles = columns // LANES

    intervals = screens.shape[1]
    packed = pl.pallas_call(
        functools.partial(pack_kernel, slots, intervals, columns),
        out_shape=jax.ShapeDtypeStruct((peers, rows, LANES), BF16),
        in_specs=[SMEM] * 2 + [VMEM] * 6,
        out_specs=VMEM,
        scratch_shapes=[
            pltpu.VMEM(((peers + 1) * rows, LANES), F32),
            pltpu.VMEM(((peers + 1) * 16, LANES), F32),
            pltpu.VMEM((items, LANES), F32),
            pltpu.SMEM((peers + 1,), jnp.int32),
        ],
        name="pack",
    )(owner[:, 0], row, baseline[None], tick[None], col[None], steps[None], positions.T, visibilities)
    received = lax.all_to_all(packed, "tile", split_axis=0, concat_axis=0, tiled=True)

    table = screens.reshape(screens.shape[0] * screens.shape[1], 8, SUB * SUB)
    total = table.shape[0]
    size = 40
    planes = pl.pallas_call(
        planes_kernel,
        out_shape=jax.ShapeDtypeStruct((total, 64, LANES), BF16),
        in_specs=[ANY],
        out_specs=ANY,
        scratch_shapes=[
            pltpu.VMEM((3, size, 8, SUB * SUB), BF16),
            pltpu.VMEM((4, 64, LANES), F32),
            pltpu.VMEM((2, size, 64, LANES), BF16),
            pltpu.SemaphoreType.DMA((3,)),
            pltpu.SemaphoreType.DMA((2,)),
        ],
        cost_estimate=pl.CostEstimate(flops=10**8, bytes_accessed=3 * 10**7, transcendentals=0),
        compiler_params=pltpu.CompilerParams(vmem_limit_bytes=56 * 1024 * 1024),
        name="screen_planes",
    )(table)

    inner, twiddle, outer = dft_tables()
    return pl.pallas_call(
        functools.partial(main_kernel, slots, intervals),
        out_shape=jax.ShapeDtypeStruct((8, STRIP, columns), F32),
        in_specs=[VMEM] + [ANY] * 5,
        out_specs=VMEM,
        scratch_shapes=[
            pltpu.VMEM((most, LANES), F32),
            pltpu.VMEM((8, wide), jnp.int32),
            pltpu.VMEM((most * KINDS, LANES), F32),
            pltpu.VMEM((most, 64, LANES), F32),
            pltpu.VMEM((2 * most, 64, LANES), BF16),
            pltpu.VMEM((2 * tiles, 8, 3 * STRIP, LANES), F32),
            pltpu.SMEM((8, wide), jnp.int32),
            pltpu.VMEM((1, channel_freq.shape[0]), F32),
            pltpu.VMEM(inner.shape, inner.dtype),
            pltpu.VMEM(twiddle.shape, twiddle.dtype),
            pltpu.VMEM(outer.shape, outer.dtype),
            pltpu.SemaphoreType.DMA,
            pltpu.SemaphoreType.DMA((2,)),
            pltpu.SemaphoreType.DMA((4,)),
        ],
        compiler_params=pltpu.CompilerParams(vmem_limit_bytes=50 * 1024 * 1024),
        name="grid_items",
    )(received, channel_freq[None, :], inner, twiddle, outer, planes)


def solution(mesh):
    return jax.shard_map(
        body,
        mesh=mesh,
        in_specs=(
            P(("band", "tile"), None, None),
            P("band", None, None, None),
            P(),
            P("band"),
            P(("band", "tile"), None),
            P(("band", "tile")),
            P(("band", "tile")),
            P(("band", "tile")),
            P(("band", "tile")),
            P(("band", "tile")),
        ),
        out_specs=P("band", "tile", None),
        check_vma=False,
    )
```

```python
import functools
import math

import jax
import jax.numpy as jnp
import numpy as np
from jax import lax
from jax.experimental import pallas as pl
from jax.experimental.pallas import tpu as pltpu
from jax.sharding import PartitionSpec as P

SUB = 32
NT = 2
BPER = 8
STRIP = 32
HALF = 16
GCOLS = 1024
LANES = 128
KINDS = 48

hour_step = 0.003
declination = -0.5

F32 = jnp.float32
BF16 = jnp.bfloat16
VMEM = pl.BlockSpec(memory_space=pltpu.VMEM)
SMEM = pl.BlockSpec(memory_space=pltpu.SMEM)
ANY = pl.BlockSpec(memory_space=pl.ANY)


def dft_tables():
    k8 = np.arange(8)
    turn = 2.0 * np.pi * np.outer(k8, k8) / 8.0
    c, s = np.cos(turn), np.sin(turn)
    eye = np.eye(4)
    inner = np.block([[np.kron(eye, c), np.kron(eye, s)], [-np.kron(eye, s), np.kron(eye, c)]])
    inner = np.concatenate([inner, inner], axis=1)
    m = np.arange(LANES) // SUB
    turn = 2.0 * np.pi * np.outer(k8, m) / 32.0
    twiddle = np.stack([np.cos(turn), -np.sin(turn)])
    b = np.arange(LANES) % SUB
    turn = 2.0 * np.pi * (np.outer(m, m) / 4.0 + np.outer(b, b) / 32.0)
    c, s = np.cos(turn) / 1024.0, np.sin(turn) / 1024.0
    outer = np.block([[c, -s], [s, c]]).astype(np.float32)
    high = outer.astype(jnp.bfloat16)
    low = (outer - high.astype(np.float32)).astype(jnp.bfloat16)
    return (
        jnp.asarray(inner.astype(jnp.bfloat16)),
        jnp.asarray(twiddle.astype(np.float32)),
        jnp.asarray(np.stack([high, low])),
    )


def pack_kernel(
    slots, intervals, columns, owner, row, base, tick, col, steps, positions, vis, out, scr, notes, record, count
):
    peers, rows, _ = out.shape
    items = vis.shape[0]
    stations = positions.shape[1]
    tiles = columns // LANES
    dims = (((1,), (1,)), ((), ()))
    best = lax.Precision.HIGHEST
    scr[...] = jnp.zeros_like(scr)
    notes[...] = jnp.zeros_like(notes)
    for t in range(peers + 1):
        count[t] = 0

    lines = jnp.concatenate([base[...], tick[...], col[...], steps[...]], axis=0).astype(F32)
    unit = lax.broadcasted_iota(jnp.int32, (items, items), 0) == lax.broadcasted_iota(jnp.int32, (items, items), 1)
    m = lax.dot_general(unit.astype(F32), lines, dims, precision=best, preferred_element_type=F32)
    m = jnp.round(m)
    baseline, time, column, valid = m[:, 0:1], m[:, 1:2], m[:, 2:3], m[:, 3:4]
    series = lax.broadcasted_iota(jnp.int32, (1, stations), 1).astype(F32)
    offsets = series * (2.0 * stations - series - 1.0) * 0.5
    one = jnp.sum((offsets <= baseline).astype(F32), axis=1, keepdims=True) - 1.0
    two = baseline - one * (2.0 * stations - one - 1.0) * 0.5 + one + 1.0
    chosen = (series == two).astype(F32) - (series == one).astype(F32)
    vector = lax.dot_general(chosen, positions[...], dims, precision=best, preferred_element_type=F32)
    high, rest = split(vector)
    rest = vector - high.astype(F32)
    middle, low = split(rest)
    tile_a = jnp.floor(column * (1.0 / LANES))
    lane_a = column - tile_a * LANES
    tile_b = jnp.floor((column - LANES // 2) * (1.0 / LANES))
    lane_b = column - LANES // 2 - tile_b * LANES
    fits = lane_a <= LANES - SUB
    values = {
        0: one,
        1: two,
        2: time,
        4: jnp.where(fits, tile_a, tile_b + tiles) + 1.0,
        5: jnp.where(fits, lane_a, lane_b),
        6: valid,
        9: jnp.floor(time * (1.0 / BPER)),
    }
    for axis in range(3):
        for k, part in enumerate((high.astype(F32), middle.astype(F32), low.astype(F32))):
            values[16 + 3 * axis + k] = part[:, axis : axis + 1]
    field = lax.broadcasted_iota(jnp.int32, (items, LANES), 1) % (LANES // 2)
    total = jnp.zeros((items, LANES), F32)
    for f, value in values.items():
        total = jnp.where(field == f, value, total)
    record[...] = total

    lane = lax.broadcasted_iota(jnp.int32, (1, LANES), 1)
    third = lane % (LANES // 2) == 3
    for i in range(items):
        o = owner[i]
        w = row[i]
        data = vis[i].astype(F32)
        common = record[i : i + 1, :]
        above = w < HALF
        near = jnp.where(above, o - 1, o + 1)
        spills = (w != HALF) & (near >= 0) & (near < peers)
        near = jnp.where(spills, near, peers)
        for target, start in ((o, w + HALF), (near, jnp.where(above, w + 48, w - HALF))):
            r = count[target]
            count[target] = jnp.where(target == peers, 0, r + 1)
            scr[pl.ds(pl.multiple_of(target * rows + r * 8, 8), 8), :] = data
            notes[pl.ds(target * 16 + r, 1), :] = jnp.where(third, start.astype(F32), common)
    lower = lax.broadcasted_iota(jnp.int32, (8, LANES), 1) < LANES // 2
    for t in range(peers):
        out[t, : slots * 8, :] = scr[t * rows : t * rows + slots * 8, :].astype(BF16)
        note = jnp.where(lower, notes[t * 16 : t * 16 + 8, :], notes[t * 16 + 8 : t * 16 + 16, :])
        out[t, slots * 8 :, :] = note.astype(BF16)


def planes_kernel(screens, out, buffer, turned, result, sems, out_sems):
    total = screens.shape[0]
    size = buffer.shape[1]
    parts = -(-total // size)
    starts = [min(part * size, total - size) for part in range(parts)]

    def load(part):
        slot = part % 3
        return pltpu.make_async_copy(screens.at[pl.ds(starts[part], size)], buffer.at[slot], sems.at[slot])

    def save(part):
        slot = part % 2
        return pltpu.make_async_copy(result.at[slot], out.at[pl.ds(starts[part], size)], out_sems.at[slot])

    load(0).start()
    if parts > 1:
        load(1).start()
    for part in range(parts):
        load(part).wait()
        if part + 2 < parts:
            load(part + 2).start()
        if part > 1:
            save(part - 2).wait()

        def some(h, _):
            for u in range(4):
                k = h * 4 + u
                data = buffer[part % 3, k].astype(F32)
                for j in range(8):
                    turned[u, pl.ds(j, 8, stride=8), :] = data[:, j * LANES : (j + 1) * LANES]
            for u in range(4):
                result[part % 2, h * 4 + u] = turned[u].astype(BF16)
            return 0

        lax.fori_loop(0, size // 4, some, 0)
        if part > 0 and starts[part] < starts[part - 1] + size:
            save(part - 1).wait()
            save(part).start()
            save(part).wait()
        else:
            save(part).start()
    overlap = parts > 1 and starts[-1] < starts[-2] + size
    if not overlap:
        if parts > 1:
            save(parts - 2).wait()
        save(parts - 1).wait()


def cos_sin_turns(x):
    x = x - jnp.round(x)
    quarter = jnp.round(x * 4.0)
    y = (x - quarter * 0.25) * (2.0 * math.pi)
    z = y * y
    s = y * (1.0 + z * (-1.0 / 6 + z * (1.0 / 120 + z * (-1.0 / 5040 + z * (1.0 / 362880)))))
    c = 1.0 + z * (-0.5 + z * (1.0 / 24 + z * (-1.0 / 720 + z * (1.0 / 40320 + z * (-1.0 / 3628800)))))
    odd = jnp.abs(quarter) == 1.0
    negative_c = (quarter == 1.0) | (jnp.abs(quarter) == 2.0)
    negative_s = (quarter == -1.0) | (jnp.abs(quarter) == 2.0)
    cos = jnp.where(odd, s, c)
    sin = jnp.where(odd, c, s)
    return jnp.where(negative_c, -cos, cos), jnp.where(negative_s, -sin, sin)


def cmul(a, b):
    return a[0] * b[0] - a[1] * b[1], a[0] * b[1] + a[1] * b[0]


def conj(a):
    return a[0], -a[1]


def both(a, b):
    rr, ii, ri, ir = a[0] * b[0], a[1] * b[1], a[0] * b[1], a[1] * b[0]
    return (rr - ii, ri + ir), (rr + ii, ir - ri)


def split(x):
    high = x.astype(BF16)
    return high, (x - high.astype(F32)).astype(BF16)


def main_kernel(
    slots, intervals, recv, freq_hbm, inner_hbm, twiddle_hbm, outer_hbm, planes,
    strip,
    meta, index, table, sky, screen, acc, place, freq, inner, twiddle, outer,
    index_sem, screen_sems, table_sems,
):
    peers, rows, _ = recv.shape
    most = meta.shape[0]
    tiles = strip.shape[2] // LANES
    lane = lax.broadcasted_iota(jnp.int32, (8, LANES), 1)
    step = (lane // (LANES // NT)).astype(F32)

    tables = [
        pltpu.make_async_copy(source, target, table_sems.at[k])
        for k, (source, target) in enumerate(
            ((freq_hbm, freq), (inner_hbm, inner), (twiddle_hbm, twiddle), (outer_hbm, outer))
        )
    ]
    for copy in tables:
        copy.start()

    halves = -(-slots // 8)
    sublane = lax.broadcasted_iota(jnp.int32, (8, LANES), 0)
    records = []
    for t in range(peers):
        chunk = recv[t, slots * 8 : slots * 8 + 8, :].astype(F32)
        for h in range(halves):
            record = pltpu.roll(chunk, LANES // 2, 1) if h else chunk
            record = jnp.where(lane == 7, float(t), record)
            records.append(jnp.where(lane == 8, (sublane + 8 * h).astype(F32), record))
    records = jnp.concatenate(records, axis=0)
    many = records.shape[0]
    filled = (records[:, 6:7] > 0.0).astype(F32)
    flags = jnp.where(lax.broadcasted_iota(jnp.int32, (many, LANES), 1) == 0, filled, 0.0).astype(BF16)
    dims = (((1,), (1,)), ((), ()))
    used = lax.dot_general(jnp.ones((8, LANES), BF16), flags, dims, preferred_element_type=F32)
    before = lax.broadcasted_iota(jnp.int32, (many, many), 0) < lax.broadcasted_iota(jnp.int32, (many, many), 1)
    rank = jnp.dot(used.astype(BF16), before.astype(F32).astype(BF16), preferred_element_type=F32)
    order = lax.broadcasted_iota(jnp.int32, (most, many), 0).astype(F32)
    pick = jnp.where((rank[0:1] == order) & (used[0:1] > 0.5), 1.0, 0.0)
    m = jnp.dot(pick.astype(BF16), records.astype(BF16), preferred_element_type=F32)
    meta[...] = m
    number = jnp.sum(filled).astype(jnp.int32)
    groups = (number + 15) // 16

    field = lax.broadcasted_iota(jnp.int32, (8, LANES), 0)
    pickers = jnp.zeros((8, LANES), F32)
    for f, source in enumerate((0, 1, 3, 4, 5, 7, 8, 9)):
        pickers = jnp.where((field == f) & (lane == source), 1.0, pickers)
    width = index.shape[1]
    wide = m.astype(BF16)
    if width > most:
        wide = jnp.concatenate([wide, jnp.zeros((width - most, LANES), BF16)], axis=0)
    fields = lax.dot_general(pickers.astype(BF16), wide, dims, preferred_element_type=F32)
    index[...] = fields.astype(jnp.int32)
    to_scalar = pltpu.make_async_copy(index, place, index_sem)
    to_scalar.start()

    tables[0].wait()

    channel = jnp.concatenate([freq[...], freq[...]], axis=1)

    def phases(g):
        here = meta[pl.ds(pl.multiple_of(g * 8, 8), 8), :]
        start = here[:, 2:3] * NT
        live = (step < here[:, 6:7]).astype(F32)
        x, y, z = [sum(here[:, 16 + 3 * a + k : 17 + 3 * a + k] for k in range(3)) for a in range(3)]
        scale = hour_step / (2.0 * math.pi)
        cos_now, sin_now = cos_sin_turns(scale * (start + step))
        cos_mid, sin_mid = cos_sin_turns(scale * (start + 0.5 * (NT - 1) + 0.0 * step))

        def track(c, s):
            u = s * x + c * y
            v = (-math.sin(declination)) * c * x + math.sin(declination) * s * y + math.cos(declination) * z
            return u, v

        u_now, v_now = track(cos_now, sin_now)
        u_mid, v_mid = track(cos_mid, sin_mid)
        du = (u_now * channel - u_mid) * (1.0 / SUB)
        dv = (v_now * channel - v_mid) * (1.0 / SUB)
        e1 = cos_sin_turns(0.5 * du)
        e2 = cmul(e1, e1)
        e3 = cmul(e2, e1)
        e4 = cmul(e2, e2)
        e8 = cmul(e4, e4)
        g1 = cos_sin_turns(dv)
        g2 = cmul(g1, g1)
        g3 = cmul(g2, g1)
        g4 = cmul(g2, g2)
        g8 = cmul(g4, g4)
        g12 = cmul(g8, g4)
        mid = (e3[0] * live, e3[1] * live)
        ups = [mid]
        for _ in range(3):
            ups.append(cmul(ups[-1], e8))
        downs = [cmul(mid, conj(e8))]
        for _ in range(3):
            downs.append(cmul(downs[-1], conj(e8)))
        row_phase = downs[::-1] + ups
        ones = (jnp.ones_like(du), jnp.zeros_like(du))
        col_phase = [conj(g4), conj(g3), conj(g2), conj(g1), ones, g1, g2, g3]
        base = pl.multiple_of(g * (KINDS * 8), 8)

        def put(kind, value):
            table[pl.ds(base + kind * 8, 8), :] = value

        for k in range(8):
            put(k, row_phase[k][0])
            put(8 + k, row_phase[k][1])
            put(16 + k, col_phase[k][0])
            put(24 + k, col_phase[k][1])
        k = 32
        for e in (e1, e3):
            plus12, minus12 = both(e, g12)
            plus4, minus4 = both(e, g4)
            for value in (minus12, minus4, plus4, plus12):
                put(k, value[0])
                put(k + 8, value[1])
                k += 1

    def all_phases(g, _):
        for h in range(2):
            phases(g * 2 + h)
        return 0

    lax.fori_loop(0, groups, all_phases, 0)
    to_scalar.wait()

    def image(g, u):
        n = g * 16 + u
        base = (2 * g + u // 8) * (KINDS * 8) + u % 8

        def rows_of(kind):
            return table[pl.ds(base + kind * 8, 8, stride=8), :]

        def row_of(kind):
            return table[pl.ds(base + kind * 8, 1), :]

        row_phase = (rows_of(0), rows_of(8))
        col_phase = (rows_of(16), rows_of(24))
        cells = [[None] * 4 for _ in range(4)]
        for k in range(8):
            mi, bb = k // 4, k % 4
            plus, minus = both(col_phase, (row_of(32 + k), row_of(40 + k)))
            cells[2 + mi][bb] = plus
            cells[1 - mi][3 - bb] = minus
        real = jnp.concatenate([cells[a][b][0] for a in range(4) for b in range(4)], axis=0)
        imag = jnp.concatenate([cells[a][b][1] for a in range(4) for b in range(4)], axis=0)
        right = jnp.concatenate([real.astype(BF16), imag.astype(BF16)], axis=1)
        block = recv[place[5, n], pl.ds(pl.multiple_of(place[6, n] * 8, 8), 8), :].astype(F32)
        reals, imags = [], []
        for p in range(4):
            value = cmul(row_phase, (block[2 * p : 2 * p + 1, :], block[2 * p + 1 : 2 * p + 2, :]))
            reals.append(value[0])
            imags.append(value[1])
        real = jnp.concatenate(reals, axis=0)
        imag = jnp.concatenate(imags, axis=0)
        left = jnp.concatenate(
            [jnp.concatenate([real, -imag], axis=1), jnp.concatenate([imag, real], axis=1)], axis=0
        )
        sky[n] = lax.dot_general(left.astype(BF16), right, dims, preferred_element_type=F32)

    batch = 16
    last = most // batch - 1

    def images(g):
        for u in range(batch):
            image(g, u)

    def fetch(g, way):
        for u in range(batch):
            for side in range(2):
                n = g * batch + u
                source = planes.at[place[side, n] * intervals + place[7, n]]
                pltpu.make_async_copy(source, screen.at[2 * n + side], screen_sems.at[way]).start()

    def land(g, way):
        here = screen.at[pl.ds(g * 2 * batch, 2 * batch)]
        pltpu.make_async_copy(planes.at[pl.ds(0, 2 * batch)], here, screen_sems.at[way]).wait()

    fetch(0, 0)
    images(0)
    for copy in tables[1:]:
        copy.wait()
    acc[:, :, STRIP : 2 * STRIP, :] = jnp.zeros((2 * tiles, 8, STRIP, LANES), F32)

    def grid(g, _):
        after = jnp.minimum(g + 1, last)
        land(g, g % 2)
        fetch(after, 1 - g % 2)
        results = []
        for u in range(batch):
            n = g * batch + u
            jones = []
            for side in range(2):
                entry = [screen[2 * n + side, 16 * k : 16 * k + 16, :].astype(F32) for k in range(4)]
                jones.append([(e[:8], e[8:]) for e in entry])
            image = sky[n]
            value = [(image[8 * p : 8 * p + 8], image[32 + 8 * p : 40 + 8 * p]) for p in range(4)]
            left, right = jones

            def add(a, b):
                return a[0] + b[0], a[1] + b[1]

            mixed = [
                add(cmul(left[2 * i], value[k]), cmul(left[2 * i + 1], value[2 + k]))
                for i in range(2)
                for k in range(2)
            ]
            corrected = [
                add(cmul(mixed[2 * i], conj(right[2 * j])), cmul(mixed[2 * i + 1], conj(right[2 * j + 1])))
                for i in range(2)
                for j in range(2)
            ]
            stacked = jnp.concatenate([c[0] for c in corrected] + [c[1] for c in corrected], axis=0)
            high, low = split(stacked)
            turned = jnp.dot(inner[...], jnp.concatenate([high, low], axis=0), preferred_element_type=F32)
            tw = (twiddle[0], twiddle[1])
            spun = [cmul((turned[8 * p : 8 * p + 8], turned[32 + 8 * p : 40 + 8 * p]), tw) for p in range(4)]
            results.append(
                jnp.concatenate(
                    [jnp.concatenate([s[0] for s in spun], axis=0), jnp.concatenate([s[1] for s in spun], axis=0)],
                    axis=1,
                )
            )
        high, low = split(jnp.concatenate(results, axis=0))
        out = jnp.dot(high, outer[0], preferred_element_type=F32)
        out += jnp.dot(high, outer[1], preferred_element_type=F32)
        out += jnp.dot(low, outer[0], preferred_element_type=F32)
        images(after)
        for u in range(batch):
            n = g * batch + u
            first = place[2, n]
            tile = place[3, n]
            shift = place[4, n]
            inside = (lane >= shift) & (lane < shift + SUB)
            cells = []
            for p in range(4):
                for r in range(2):
                    cell = out[u * 32 + 8 * p : u * 32 + 8 * p + 8, r * LANES : (r + 1) * LANES]
                    parts = []
                    for k4 in range(4):
                        turn = (shift + (LANES - SUB * k4)) % LANES
                        parts.append(jnp.where(inside, pltpu.roll(cell, turn, 1), 0.0))
                    cells.append(jnp.concatenate(parts, axis=0))
            spot = (tile, slice(None), pl.ds(first, SUB), slice(None))
            acc[spot] = acc[spot] + jnp.stack(cells)
        return 0

    lax.fori_loop(0, groups, grid, 0)
    land(jnp.minimum(groups, last), groups % 2)

    half = lax.broadcasted_iota(jnp.int32, (STRIP, LANES), 1) < LANES // 2
    mine = slice(STRIP, 2 * STRIP)
    for plane_at in range(8):
        behind = None
        for t in range(tiles):
            value = acc[1 + t, plane_at, mine, :]
            turned = None
            if t < tiles - 1:
                turned = pltpu.roll(acc[1 + tiles + t, plane_at, mine, :], LANES // 2, 1)
                value = value + jnp.where(half, 0.0, turned)
            if behind is not None:
                value = value + jnp.where(half, behind, 0.0)
            behind = turned
            strip[plane_at, :, t * LANES : (t + 1) * LANES] = value


def body(visibilities, screens, positions, channel_freq, owner, baseline, tick, row, col, steps):
    peers = lax.axis_size("tile")
    items = visibilities.shape[0]
    slots = 3 * max(2, 2 * items // peers)
    rows = slots * 8 + 8
    most = -(-peers * slots // 8) * 8
    wide = -(-most // LANES) * LANES
    columns = GCOLS
    tiles = columns // LANES

    intervals = screens.shape[1]
    packed = pl.pallas_call(
        functools.partial(pack_kernel, slots, intervals, columns),
        out_shape=jax.ShapeDtypeStruct((peers, rows, LANES), BF16),
        in_specs=[SMEM] * 2 + [VMEM] * 6,
        out_specs=VMEM,
        scratch_shapes=[
            pltpu.VMEM(((peers + 1) * rows, LANES), F32),
            pltpu.VMEM(((peers + 1) * 16, LANES), F32),
            pltpu.VMEM((items, LANES), F32),
            pltpu.SMEM((peers + 1,), jnp.int32),
        ],
        name="pack",
    )(owner[:, 0], row, baseline[None], tick[None], col[None], steps[None], positions.T, visibilities)
    received = lax.all_to_all(packed, "tile", split_axis=0, concat_axis=0, tiled=True)

    table = screens.reshape(screens.shape[0] * screens.shape[1], 8, SUB * SUB)
    total = table.shape[0]
    size = 40
    planes = pl.pallas_call(
        planes_kernel,
        out_shape=jax.ShapeDtypeStruct((total, 64, LANES), BF16),
        in_specs=[ANY],
        out_specs=ANY,
        scratch_shapes=[
            pltpu.VMEM((3, size, 8, SUB * SUB), BF16),
            pltpu.VMEM((4, 64, LANES), F32),
            pltpu.VMEM((2, size, 64, LANES), BF16),
            pltpu.SemaphoreType.DMA((3,)),
            pltpu.SemaphoreType.DMA((2,)),
        ],
        cost_estimate=pl.CostEstimate(flops=10**8, bytes_accessed=3 * 10**7, transcendentals=0),
        compiler_params=pltpu.CompilerParams(vmem_limit_bytes=56 * 1024 * 1024),
        name="screen_planes",
    )(table)

    inner, twiddle, outer = dft_tables()
    return pl.pallas_call(
        functools.partial(main_kernel, slots, intervals),
        out_shape=jax.ShapeDtypeStruct((8, STRIP, columns), F32),
        in_specs=[VMEM] + [ANY] * 5,
        out_specs=VMEM,
        scratch_shapes=[
            pltpu.VMEM((most, LANES), F32),
            pltpu.VMEM((8, wide), jnp.int32),
            pltpu.VMEM((most * KINDS, LANES), F32),
            pltpu.VMEM((most, 64, LANES), F32),
            pltpu.VMEM((2 * most, 64, LANES), BF16),
            pltpu.VMEM((2 * tiles, 8, 3 * STRIP, LANES), F32),
            pltpu.SMEM((8, wide), jnp.int32),
            pltpu.VMEM((1, channel_freq.shape[0]), F32),
            pltpu.VMEM(inner.shape, inner.dtype),
            pltpu.VMEM(twiddle.shape, twiddle.dtype),
            pltpu.VMEM(outer.shape, outer.dtype),
            pltpu.SemaphoreType.DMA,
            pltpu.SemaphoreType.DMA((2,)),
            pltpu.SemaphoreType.DMA((4,)),
        ],
        compiler_params=pltpu.CompilerParams(vmem_limit_bytes=50 * 1024 * 1024),
        name="grid_items",
    )(received, channel_freq[None, :], inner, twiddle, outer, planes)


def solution(mesh):
    return jax.shard_map(
        body,
        mesh=mesh,
        in_specs=(
            P(("band", "tile"), None, None),
            P("band", None, None, None),
            P(),
            P("band"),
            P(("band", "tile"), None),
            P(("band", "tile")),
            P(("band", "tile")),
            P(("band", "tile")),
            P(("band", "tile")),
            P(("band", "tile")),
        ),
        out_specs=P("band", "tile", None),
        check_vma=False,
    )
```

```python
import functools
import math

import jax
import jax.numpy as jnp
import numpy as np
from jax import lax
from jax.experimental import pallas as pl
from jax.experimental.pallas import tpu as pltpu
from jax.sharding import PartitionSpec as P

SUB = 32
NT = 2
BPER = 8
STRIP = 32
HALF = 16
GCOLS = 1024
LANES = 128
KINDS = 48

hour_step = 0.003
declination = -0.5

F32 = jnp.float32
BF16 = jnp.bfloat16
VMEM = pl.BlockSpec(memory_space=pltpu.VMEM)
SMEM = pl.BlockSpec(memory_space=pltpu.SMEM)
ANY = pl.BlockSpec(memory_space=pl.ANY)


def dft_tables():
    k8 = np.arange(8)
    turn = 2.0 * np.pi * np.outer(k8, k8) / 8.0
    c, s = np.cos(turn), np.sin(turn)
    eye = np.eye(4)
    inner = np.block([[np.kron(eye, c), np.kron(eye, s)], [-np.kron(eye, s), np.kron(eye, c)]])
    inner = np.concatenate([inner, inner], axis=1)
    m = np.arange(LANES) // SUB
    turn = 2.0 * np.pi * np.outer(k8, m) / 32.0
    twiddle = np.stack([np.cos(turn), -np.sin(turn)])
    b = np.arange(LANES) % SUB
    turn = 2.0 * np.pi * (np.outer(m, m) / 4.0 + np.outer(b, b) / 32.0)
    c, s = np.cos(turn) / 1024.0, np.sin(turn) / 1024.0
    outer = np.block([[c, -s], [s, c]]).astype(np.float32)
    high = outer.astype(jnp.bfloat16)
    low = (outer - high.astype(np.float32)).astype(jnp.bfloat16)
    return (
        jnp.asarray(inner.astype(jnp.bfloat16)),
        jnp.asarray(twiddle.astype(np.float32)),
        jnp.asarray(np.stack([high, low])),
    )


def pack_kernel(
    slots, intervals, columns, owner, row, base, tick, col, steps, positions, vis, out, scr, notes, record, count
):
    peers, rows, _ = out.shape
    items = vis.shape[0]
    stations = positions.shape[1]
    tiles = columns // LANES
    dims = (((1,), (1,)), ((), ()))
    best = lax.Precision.HIGHEST
    scr[...] = jnp.zeros_like(scr)
    notes[...] = jnp.zeros_like(notes)
    for t in range(peers + 1):
        count[t] = 0

    lines = jnp.concatenate([base[...], tick[...], col[...], steps[...]], axis=0).astype(F32)
    unit = lax.broadcasted_iota(jnp.int32, (items, items), 0) == lax.broadcasted_iota(jnp.int32, (items, items), 1)
    m = lax.dot_general(unit.astype(F32), lines, dims, precision=best, preferred_element_type=F32)
    m = jnp.round(m)
    baseline, time, column, valid = m[:, 0:1], m[:, 1:2], m[:, 2:3], m[:, 3:4]
    series = lax.broadcasted_iota(jnp.int32, (1, stations), 1).astype(F32)
    offsets = series * (2.0 * stations - series - 1.0) * 0.5
    one = jnp.sum((offsets <= baseline).astype(F32), axis=1, keepdims=True) - 1.0
    two = baseline - one * (2.0 * stations - one - 1.0) * 0.5 + one + 1.0
    chosen = (series == two).astype(F32) - (series == one).astype(F32)
    vector = lax.dot_general(chosen, positions[...], dims, precision=best, preferred_element_type=F32)
    high, rest = split(vector)
    rest = vector - high.astype(F32)
    middle, low = split(rest)
    tile_a = jnp.floor(column * (1.0 / LANES))
    lane_a = column - tile_a * LANES
    tile_b = jnp.floor((column - LANES // 2) * (1.0 / LANES))
    lane_b = column - LANES // 2 - tile_b * LANES
    fits = lane_a <= LANES - SUB
    values = {
        0: one,
        1: two,
        2: time,
        4: jnp.where(fits, tile_a, tile_b + tiles) + 1.0,
        5: jnp.where(fits, lane_a, lane_b),
        6: valid,
        9: jnp.floor(time * (1.0 / BPER)),
    }
    for axis in range(3):
        for k, part in enumerate((high.astype(F32), middle.astype(F32), low.astype(F32))):
            values[16 + 3 * axis + k] = part[:, axis : axis + 1]
    field = lax.broadcasted_iota(jnp.int32, (items, LANES), 1) % (LANES // 2)
    total = jnp.zeros((items, LANES), F32)
    for f, value in values.items():
        total = jnp.where(field == f, value, total)
    record[...] = total

    lane = lax.broadcasted_iota(jnp.int32, (1, LANES), 1)
    third = lane % (LANES // 2) == 3
    for i in range(items):
        o = owner[i]
        w = row[i]
        data = vis[i].astype(F32)
        common = record[i : i + 1, :]
        above = w < HALF
        near = jnp.where(above, o - 1, o + 1)
        spills = (w != HALF) & (near >= 0) & (near < peers)
        near = jnp.where(spills, near, peers)
        for target, start in ((o, w + HALF), (near, jnp.where(above, w + 48, w - HALF))):
            r = count[target]
            count[target] = jnp.where(target == peers, 0, r + 1)
            scr[pl.ds(pl.multiple_of(target * rows + r * 8, 8), 8), :] = data
            notes[pl.ds(target * 16 + r, 1), :] = jnp.where(third, start.astype(F32), common)
    lower = lax.broadcasted_iota(jnp.int32, (8, LANES), 1) < LANES // 2
    for t in range(peers):
        out[t, : slots * 8, :] = scr[t * rows : t * rows + slots * 8, :].astype(BF16)
        note = jnp.where(lower, notes[t * 16 : t * 16 + 8, :], notes[t * 16 + 8 : t * 16 + 16, :])
        out[t, slots * 8 :, :] = note.astype(BF16)


def planes_kernel(screens, out, buffer, turned, result, sems, out_sems):
    total = screens.shape[0]
    size = buffer.shape[1]
    parts = -(-total // size)
    starts = [min(part * size, total - size) for part in range(parts)]

    def load(part):
        slot = part % 3
        return pltpu.make_async_copy(screens.at[pl.ds(starts[part], size)], buffer.at[slot], sems.at[slot])

    def save(part):
        slot = part % 2
        return pltpu.make_async_copy(result.at[slot], out.at[pl.ds(starts[part], size)], out_sems.at[slot])

    load(0).start()
    if parts > 1:
        load(1).start()
    for part in range(parts):
        load(part).wait()
        if part + 2 < parts:
            load(part + 2).start()
        if part > 1:
            save(part - 2).wait()

        def some(h, _):
            for u in range(4):
                k = h * 4 + u
                data = buffer[part % 3, k].astype(F32)
                for j in range(8):
                    turned[u, pl.ds(j, 8, stride=8), :] = data[:, j * LANES : (j + 1) * LANES]
            for u in range(4):
                result[part % 2, h * 4 + u] = turned[u].astype(BF16)
            return 0

        lax.fori_loop(0, size // 4, some, 0)
        if part > 0 and starts[part] < starts[part - 1] + size:
            save(part - 1).wait()
            save(part).start()
            save(part).wait()
        else:
            save(part).start()
    overlap = parts > 1 and starts[-1] < starts[-2] + size
    if not overlap:
        if parts > 1:
            save(parts - 2).wait()
        save(parts - 1).wait()


def cos_sin_turns(x):
    x = x - jnp.round(x)
    quarter = jnp.round(x * 4.0)
    y = (x - quarter * 0.25) * (2.0 * math.pi)
    z = y * y
    s = y * (1.0 + z * (-1.0 / 6 + z * (1.0 / 120 + z * (-1.0 / 5040 + z * (1.0 / 362880)))))
    c = 1.0 + z * (-0.5 + z * (1.0 / 24 + z * (-1.0 / 720 + z * (1.0 / 40320 + z * (-1.0 / 3628800)))))
    odd = jnp.abs(quarter) == 1.0
    negative_c = (quarter == 1.0) | (jnp.abs(quarter) == 2.0)
    negative_s = (quarter == -1.0) | (jnp.abs(quarter) == 2.0)
    cos = jnp.where(odd, s, c)
    sin = jnp.where(odd, c, s)
    return jnp.where(negative_c, -cos, cos), jnp.where(negative_s, -sin, sin)


def cmul(a, b):
    return a[0] * b[0] - a[1] * b[1], a[0] * b[1] + a[1] * b[0]


def conj(a):
    return a[0], -a[1]


def both(a, b):
    rr, ii, ri, ir = a[0] * b[0], a[1] * b[1], a[0] * b[1], a[1] * b[0]
    return (rr - ii, ri + ir), (rr + ii, ir - ri)


def split(x):
    high = x.astype(BF16)
    return high, (x - high.astype(F32)).astype(BF16)


def main_kernel(
    slots, intervals, recv, freq_hbm, inner_hbm, twiddle_hbm, outer_hbm, planes,
    strip,
    meta, index, table, sky, screen, acc, place, freq, inner, twiddle, outer,
    index_sem, screen_sems, table_sems,
):
    peers, rows, _ = recv.shape
    most = meta.shape[0]
    tiles = strip.shape[2] // LANES
    lane = lax.broadcasted_iota(jnp.int32, (8, LANES), 1)
    step = (lane // (LANES // NT)).astype(F32)

    tables = [
        pltpu.make_async_copy(source, target, table_sems.at[k])
        for k, (source, target) in enumerate(
            ((freq_hbm, freq), (inner_hbm, inner), (twiddle_hbm, twiddle), (outer_hbm, outer))
        )
    ]
    for copy in tables:
        copy.start()

    halves = -(-slots // 8)
    sublane = lax.broadcasted_iota(jnp.int32, (8, LANES), 0)
    records = []
    for t in range(peers):
        chunk = recv[t, slots * 8 : slots * 8 + 8, :].astype(F32)
        for h in range(halves):
            record = pltpu.roll(chunk, LANES // 2, 1) if h else chunk
            record = jnp.where(lane == 7, float(t), record)
            records.append(jnp.where(lane == 8, (sublane + 8 * h).astype(F32), record))
    records = jnp.concatenate(records, axis=0)
    many = records.shape[0]
    filled = (records[:, 6:7] > 0.0).astype(F32)
    flags = jnp.where(lax.broadcasted_iota(jnp.int32, (many, LANES), 1) == 0, filled, 0.0).astype(BF16)
    dims = (((1,), (1,)), ((), ()))
    used = lax.dot_general(jnp.ones((8, LANES), BF16), flags, dims, preferred_element_type=F32)
    before = lax.broadcasted_iota(jnp.int32, (many, many), 0) < lax.broadcasted_iota(jnp.int32, (many, many), 1)
    rank = jnp.dot(used.astype(BF16), before.astype(F32).astype(BF16), preferred_element_type=F32)
    order = lax.broadcasted_iota(jnp.int32, (most, many), 0).astype(F32)
    pick = jnp.where((rank[0:1] == order) & (used[0:1] > 0.5), 1.0, 0.0)
    m = jnp.dot(pick.astype(BF16), records.astype(BF16), preferred_element_type=F32)
    meta[...] = m
    number = jnp.sum(filled).astype(jnp.int32)
    groups = jnp.maximum((number + 15) // 16, 1)

    field = lax.broadcasted_iota(jnp.int32, (8, LANES), 0)
    pickers = jnp.zeros((8, LANES), F32)
    for f, source in enumerate((0, 1, 3, 4, 5, 7, 8, 9)):
        pickers = jnp.where((field == f) & (lane == source), 1.0, pickers)
    width = index.shape[1]
    wide = m.astype(BF16)
    if width > most:
        wide = jnp.concatenate([wide, jnp.zeros((width - most, LANES), BF16)], axis=0)
    fields = lax.dot_general(pickers.astype(BF16), wide, dims, preferred_element_type=F32)
    index[...] = fields.astype(jnp.int32)
    to_scalar = pltpu.make_async_copy(index, place, index_sem)
    to_scalar.start()

    tables[0].wait()

    channel = jnp.concatenate([freq[...], freq[...]], axis=1)

    def phases(g):
        here = meta[pl.ds(pl.multiple_of(g * 8, 8), 8), :]
        start = here[:, 2:3] * NT
        live = (step < here[:, 6:7]).astype(F32)
        x, y, z = [sum(here[:, 16 + 3 * a + k : 17 + 3 * a + k] for k in range(3)) for a in range(3)]
        scale = hour_step / (2.0 * math.pi)
        cos_now, sin_now = cos_sin_turns(scale * (start + step))
        cos_mid, sin_mid = cos_sin_turns(scale * (start + 0.5 * (NT - 1) + 0.0 * step))

        def track(c, s):
            u = s * x + c * y
            v = (-math.sin(declination)) * c * x + math.sin(declination) * s * y + math.cos(declination) * z
            return u, v

        u_now, v_now = track(cos_now, sin_now)
        u_mid, v_mid = track(cos_mid, sin_mid)
        du = (u_now * channel - u_mid) * (1.0 / SUB)
        dv = (v_now * channel - v_mid) * (1.0 / SUB)
        e1 = cos_sin_turns(0.5 * du)
        e2 = cmul(e1, e1)
        e3 = cmul(e2, e1)
        e4 = cmul(e2, e2)
        e8 = cmul(e4, e4)
        g1 = cos_sin_turns(dv)
        g2 = cmul(g1, g1)
        g3 = cmul(g2, g1)
        g4 = cmul(g2, g2)
        g8 = cmul(g4, g4)
        g12 = cmul(g8, g4)
        mid = (e3[0] * live, e3[1] * live)
        ups = [mid]
        for _ in range(3):
            ups.append(cmul(ups[-1], e8))
        downs = [cmul(mid, conj(e8))]
        for _ in range(3):
            downs.append(cmul(downs[-1], conj(e8)))
        row_phase = downs[::-1] + ups
        ones = (jnp.ones_like(du), jnp.zeros_like(du))
        col_phase = [conj(g4), conj(g3), conj(g2), conj(g1), ones, g1, g2, g3]
        base = pl.multiple_of(g * (KINDS * 8), 8)

        def put(kind, value):
            table[pl.ds(base + kind * 8, 8), :] = value

        for k in range(8):
            put(k, row_phase[k][0])
            put(8 + k, row_phase[k][1])
            put(16 + k, col_phase[k][0])
            put(24 + k, col_phase[k][1])
        k = 32
        for e in (e1, e3):
            plus12, minus12 = both(e, g12)
            plus4, minus4 = both(e, g4)
            for value in (minus12, minus4, plus4, plus12):
                put(k, value[0])
                put(k + 8, value[1])
                k += 1

    def all_phases(g, _):
        for h in range(2):
            phases(g * 2 + h)
        return 0

    lax.fori_loop(0, groups, all_phases, 0)
    to_scalar.wait()

    def image(g, u):
        n = g * 16 + u
        base = (2 * g + u // 8) * (KINDS * 8) + u % 8

        def rows_of(kind):
            return table[pl.ds(base + kind * 8, 8, stride=8), :]

        def row_of(kind):
            return table[pl.ds(base + kind * 8, 1), :]

        row_phase = (rows_of(0), rows_of(8))
        col_phase = (rows_of(16), rows_of(24))
        cells = [[None] * 4 for _ in range(4)]
        for k in range(8):
            mi, bb = k // 4, k % 4
            plus, minus = both(col_phase, (row_of(32 + k), row_of(40 + k)))
            cells[2 + mi][bb] = plus
            cells[1 - mi][3 - bb] = minus
        real = jnp.concatenate([cells[a][b][0] for a in range(4) for b in range(4)], axis=0)
        imag = jnp.concatenate([cells[a][b][1] for a in range(4) for b in range(4)], axis=0)
        right = jnp.concatenate([real.astype(BF16), imag.astype(BF16)], axis=1)
        block = recv[place[5, n], pl.ds(pl.multiple_of(place[6, n] * 8, 8), 8), :].astype(F32)
        reals, imags = [], []
        for p in range(4):
            value = cmul(row_phase, (block[2 * p : 2 * p + 1, :], block[2 * p + 1 : 2 * p + 2, :]))
            reals.append(value[0])
            imags.append(value[1])
        real = jnp.concatenate(reals, axis=0)
        imag = jnp.concatenate(imags, axis=0)
        left = jnp.concatenate(
            [jnp.concatenate([real, -imag], axis=1), jnp.concatenate([imag, real], axis=1)], axis=0
        )
        sky[n] = lax.dot_general(left.astype(BF16), right, dims, preferred_element_type=F32)

    batch = 16

    def images(g):
        for u in range(batch):
            image(g, u)

    def fetch(g, way):
        for u in range(batch):
            for side in range(2):
                n = g * batch + u
                source = planes.at[place[side, n] * intervals + place[7, n]]
                pltpu.make_async_copy(source, screen.at[2 * n + side], screen_sems.at[way]).start()

    def land(g, way):
        here = screen.at[pl.ds(g * 2 * batch, 2 * batch)]
        pltpu.make_async_copy(planes.at[pl.ds(0, 2 * batch)], here, screen_sems.at[way]).wait()

    fetch(0, 0)
    images(0)
    for copy in tables[1:]:
        copy.wait()
    acc[:, :, STRIP : 2 * STRIP, :] = jnp.zeros((2 * tiles, 8, STRIP, LANES), F32)

    def settle(g, size, ahead):
        results = []
        for u in range(size):
            n = g * batch + u
            jones = []
            for side in range(2):
                entry = [screen[2 * n + side, 16 * k : 16 * k + 16, :].astype(F32) for k in range(4)]
                jones.append([(e[:8], e[8:]) for e in entry])
            image = sky[n]
            value = [(image[8 * p : 8 * p + 8], image[32 + 8 * p : 40 + 8 * p]) for p in range(4)]
            left, right = jones

            def add(a, b):
                return a[0] + b[0], a[1] + b[1]

            mixed = [
                add(cmul(left[2 * i], value[k]), cmul(left[2 * i + 1], value[2 + k]))
                for i in range(2)
                for k in range(2)
            ]
            corrected = [
                add(cmul(mixed[2 * i], conj(right[2 * j])), cmul(mixed[2 * i + 1], conj(right[2 * j + 1])))
                for i in range(2)
                for j in range(2)
            ]
            stacked = jnp.concatenate([c[0] for c in corrected] + [c[1] for c in corrected], axis=0)
            high, low = split(stacked)
            turned = jnp.dot(inner[...], jnp.concatenate([high, low], axis=0), preferred_element_type=F32)
            tw = (twiddle[0], twiddle[1])
            spun = [cmul((turned[8 * p : 8 * p + 8], turned[32 + 8 * p : 40 + 8 * p]), tw) for p in range(4)]
            results.append(
                jnp.concatenate(
                    [jnp.concatenate([s[0] for s in spun], axis=0), jnp.concatenate([s[1] for s in spun], axis=0)],
                    axis=1,
                )
            )
        high, low = split(jnp.concatenate(results, axis=0))
        out = jnp.dot(high, outer[0], preferred_element_type=F32)
        out += jnp.dot(high, outer[1], preferred_element_type=F32)
        out += jnp.dot(low, outer[0], preferred_element_type=F32)
        if ahead is not None:
            images(ahead)
        for u in range(size):
            n = g * batch + u
            first = place[2, n]
            tile = place[3, n]
            shift = place[4, n]
            inside = (lane >= shift) & (lane < shift + SUB)
            cells = []
            for p in range(4):
                for r in range(2):
                    cell = out[u * 32 + 8 * p : u * 32 + 8 * p + 8, r * LANES : (r + 1) * LANES]
                    parts = []
                    for k4 in range(4):
                        turn = (shift + (LANES - SUB * k4)) % LANES
                        parts.append(jnp.where(inside, pltpu.roll(cell, turn, 1), 0.0))
                    cells.append(jnp.concatenate(parts, axis=0))
            spot = (tile, slice(None), pl.ds(first, SUB), slice(None))
            acc[spot] = acc[spot] + jnp.stack(cells)

    def grid(g, _):
        land(g, g % 2)
        fetch(g + 1, 1 - g % 2)
        settle(g, batch, g + 1)
        return 0

    end = groups - 1
    lax.fori_loop(0, end, grid, 0)
    land(end, end % 2)
    few = number - end * batch <= batch // 2

    @pl.when(few)
    def _():
        settle(end, batch // 2, None)

    @pl.when(jnp.logical_not(few))
    def _():
        settle(end, batch, None)


    half = lax.broadcasted_iota(jnp.int32, (STRIP, LANES), 1) < LANES // 2
    mine = slice(STRIP, 2 * STRIP)
    for plane_at in range(8):
        behind = None
        for t in range(tiles):
            value = acc[1 + t, plane_at, mine, :]
            turned = None
            if t < tiles - 1:
                turned = pltpu.roll(acc[1 + tiles + t, plane_at, mine, :], LANES // 2, 1)
                value = value + jnp.where(half, 0.0, turned)
            if behind is not None:
                value = value + jnp.where(half, behind, 0.0)
            behind = turned
            strip[plane_at, :, t * LANES : (t + 1) * LANES] = value


def body(visibilities, screens, positions, channel_freq, owner, baseline, tick, row, col, steps):
    peers = lax.axis_size("tile")
    items = visibilities.shape[0]
    slots = 3 * max(2, 2 * items // peers)
    rows = slots * 8 + 8
    most = -(-peers * slots // 8) * 8
    wide = -(-most // LANES) * LANES
    columns = GCOLS
    tiles = columns // LANES

    intervals = screens.shape[1]
    packed = pl.pallas_call(
        functools.partial(pack_kernel, slots, intervals, columns),
        out_shape=jax.ShapeDtypeStruct((peers, rows, LANES), BF16),
        in_specs=[SMEM] * 2 + [VMEM] * 6,
        out_specs=VMEM,
        scratch_shapes=[
            pltpu.VMEM(((peers + 1) * rows, LANES), F32),
            pltpu.VMEM(((peers + 1) * 16, LANES), F32),
            pltpu.VMEM((items, LANES), F32),
            pltpu.SMEM((peers + 1,), jnp.int32),
        ],
        name="pack",
    )(owner[:, 0], row, baseline[None], tick[None], col[None], steps[None], positions.T, visibilities)
    received = lax.all_to_all(packed, "tile", split_axis=0, concat_axis=0, tiled=True)

    table = screens.reshape(screens.shape[0] * screens.shape[1], 8, SUB * SUB)
    total = table.shape[0]
    size = 40
    planes = pl.pallas_call(
        planes_kernel,
        out_shape=jax.ShapeDtypeStruct((total, 64, LANES), BF16),
        in_specs=[ANY],
        out_specs=ANY,
        scratch_shapes=[
            pltpu.VMEM((3, size, 8, SUB * SUB), BF16),
            pltpu.VMEM((4, 64, LANES), F32),
            pltpu.VMEM((2, size, 64, LANES), BF16),
            pltpu.SemaphoreType.DMA((3,)),
            pltpu.SemaphoreType.DMA((2,)),
        ],
        cost_estimate=pl.CostEstimate(flops=10**8, bytes_accessed=3 * 10**7, transcendentals=0),
        compiler_params=pltpu.CompilerParams(vmem_limit_bytes=56 * 1024 * 1024),
        name="screen_planes",
    )(table)

    inner, twiddle, outer = dft_tables()
    return pl.pallas_call(
        functools.partial(main_kernel, slots, intervals),
        out_shape=jax.ShapeDtypeStruct((8, STRIP, columns), F32),
        in_specs=[VMEM] + [ANY] * 5,
        out_specs=VMEM,
        scratch_shapes=[
            pltpu.VMEM((most, LANES), F32),
            pltpu.VMEM((8, wide), jnp.int32),
            pltpu.VMEM((most * KINDS, LANES), F32),
            pltpu.VMEM((most, 64, LANES), F32),
            pltpu.VMEM((2 * most, 64, LANES), BF16),
            pltpu.VMEM((2 * tiles, 8, 3 * STRIP, LANES), F32),
            pltpu.SMEM((8, wide), jnp.int32),
            pltpu.VMEM((1, channel_freq.shape[0]), F32),
            pltpu.VMEM(inner.shape, inner.dtype),
            pltpu.VMEM(twiddle.shape, twiddle.dtype),
            pltpu.VMEM(outer.shape, outer.dtype),
            pltpu.SemaphoreType.DMA,
            pltpu.SemaphoreType.DMA((2,)),
            pltpu.SemaphoreType.DMA((4,)),
        ],
        compiler_params=pltpu.CompilerParams(vmem_limit_bytes=50 * 1024 * 1024),
        name="grid_items",
    )(received, channel_freq[None, :], inner, twiddle, outer, planes)


def solution(mesh):
    return jax.shard_map(
        body,
        mesh=mesh,
        in_specs=(
            P(("band", "tile"), None, None),
            P("band", None, None, None),
            P(),
            P("band"),
            P(("band", "tile"), None),
            P(("band", "tile")),
            P(("band", "tile")),
            P(("band", "tile")),
            P(("band", "tile")),
            P(("band", "tile")),
        ),
        out_specs=P("band", "tile", None),
        check_vma=False,
    )
```

```python
import functools
import math

import jax
import jax.numpy as jnp
import numpy as np
from jax import lax
from jax.experimental import pallas as pl
from jax.experimental.pallas import tpu as pltpu
from jax.sharding import PartitionSpec as P

SUB = 32
NT = 2
BPER = 8
STRIP = 32
HALF = 16
GCOLS = 1024
LANES = 128
KINDS = 48

hour_step = 0.003
declination = -0.5

F32 = jnp.float32
BF16 = jnp.bfloat16
VMEM = pl.BlockSpec(memory_space=pltpu.VMEM)
SMEM = pl.BlockSpec(memory_space=pltpu.SMEM)
ANY = pl.BlockSpec(memory_space=pl.ANY)


def dft_tables():
    k8 = np.arange(8)
    turn = 2.0 * np.pi * np.outer(k8, k8) / 8.0
    c, s = np.cos(turn), np.sin(turn)
    eye = np.eye(4)
    inner = np.block([[np.kron(eye, c), np.kron(eye, s)], [-np.kron(eye, s), np.kron(eye, c)]])
    inner = np.concatenate([inner, inner], axis=1)
    m = np.arange(LANES) // SUB
    turn = 2.0 * np.pi * np.outer(k8, m) / 32.0
    twiddle = np.stack([np.cos(turn), -np.sin(turn)])
    b = np.arange(LANES) % SUB
    turn = 2.0 * np.pi * (np.outer(m, m) / 4.0 + np.outer(b, b) / 32.0)
    c, s = np.cos(turn) / 1024.0, np.sin(turn) / 1024.0
    outer = np.block([[c, -s], [s, c]]).astype(np.float32)
    high = outer.astype(jnp.bfloat16)
    low = (outer - high.astype(np.float32)).astype(jnp.bfloat16)
    return (
        jnp.asarray(inner.astype(jnp.bfloat16)),
        jnp.asarray(twiddle.astype(np.float32)),
        jnp.asarray(np.stack([high, low])),
    )


def pack_kernel(
    slots, intervals, columns, owner, row, base, tick, col, steps, positions, vis, out, scr, notes, record, count
):
    peers, rows, _ = out.shape
    items = vis.shape[0]
    stations = positions.shape[1]
    tiles = columns // LANES
    dims = (((1,), (1,)), ((), ()))
    best = lax.Precision.HIGHEST
    scr[...] = jnp.zeros_like(scr)
    notes[...] = jnp.zeros_like(notes)
    for t in range(peers + 1):
        count[t] = 0

    lines = jnp.concatenate([base[...], tick[...], col[...], steps[...]], axis=0).astype(F32)
    unit = lax.broadcasted_iota(jnp.int32, (items, items), 0) == lax.broadcasted_iota(jnp.int32, (items, items), 1)
    m = lax.dot_general(unit.astype(F32), lines, dims, precision=best, preferred_element_type=F32)
    m = jnp.round(m)
    baseline, time, column, valid = m[:, 0:1], m[:, 1:2], m[:, 2:3], m[:, 3:4]
    series = lax.broadcasted_iota(jnp.int32, (1, stations), 1).astype(F32)
    offsets = series * (2.0 * stations - series - 1.0) * 0.5
    one = jnp.sum((offsets <= baseline).astype(F32), axis=1, keepdims=True) - 1.0
    two = baseline - one * (2.0 * stations - one - 1.0) * 0.5 + one + 1.0
    chosen = (series == two).astype(F32) - (series == one).astype(F32)
    vector = lax.dot_general(chosen, positions[...], dims, precision=best, preferred_element_type=F32)
    high, rest = split(vector)
    rest = vector - high.astype(F32)
    middle, low = split(rest)
    tile_a = jnp.floor(column * (1.0 / LANES))
    lane_a = column - tile_a * LANES
    tile_b = jnp.floor((column - LANES // 2) * (1.0 / LANES))
    lane_b = column - LANES // 2 - tile_b * LANES
    fits = lane_a <= LANES - SUB
    values = {
        0: one,
        1: two,
        2: time,
        4: jnp.where(fits, tile_a, tile_b + tiles) + 1.0,
        5: jnp.where(fits, lane_a, lane_b),
        6: valid,
        9: jnp.floor(time * (1.0 / BPER)),
    }
    for axis in range(3):
        for k, part in enumerate((high.astype(F32), middle.astype(F32), low.astype(F32))):
            values[16 + 3 * axis + k] = part[:, axis : axis + 1]
    field = lax.broadcasted_iota(jnp.int32, (items, LANES), 1) % (LANES // 2)
    total = jnp.zeros((items, LANES), F32)
    for f, value in values.items():
        total = jnp.where(field == f, value, total)
    record[...] = total

    lane = lax.broadcasted_iota(jnp.int32, (1, LANES), 1)
    third = lane % (LANES // 2) == 3
    for i in range(items):
        o = owner[i]
        w = row[i]
        data = vis[i].astype(F32)
        common = record[i : i + 1, :]
        above = w < HALF
        near = jnp.where(above, o - 1, o + 1)
        spills = (w != HALF) & (near >= 0) & (near < peers)
        near = jnp.where(spills, near, peers)
        for target, start in ((o, w + HALF), (near, jnp.where(above, w + 48, w - HALF))):
            r = count[target]
            count[target] = jnp.where(target == peers, 0, r + 1)
            scr[pl.ds(pl.multiple_of(target * rows + r * 8, 8), 8), :] = data
            notes[pl.ds(target * 16 + r, 1), :] = jnp.where(third, start.astype(F32), common)
    lower = lax.broadcasted_iota(jnp.int32, (8, LANES), 1) < LANES // 2
    for t in range(peers):
        out[t, : slots * 8, :] = scr[t * rows : t * rows + slots * 8, :].astype(BF16)
        note = jnp.where(lower, notes[t * 16 : t * 16 + 8, :], notes[t * 16 + 8 : t * 16 + 16, :])
        out[t, slots * 8 :, :] = note.astype(BF16)


def planes_kernel(screens, out, buffer, turned, result, sems, out_sems):
    total = screens.shape[0]
    size = buffer.shape[1]
    parts = -(-total // size)
    starts = [min(part * size, total - size) for part in range(parts)]

    def load(part):
        slot = part % 3
        return pltpu.make_async_copy(screens.at[pl.ds(starts[part], size)], buffer.at[slot], sems.at[slot])

    def save(part):
        slot = part % 2
        return pltpu.make_async_copy(result.at[slot], out.at[pl.ds(starts[part], size)], out_sems.at[slot])

    load(0).start()
    if parts > 1:
        load(1).start()
    for part in range(parts):
        load(part).wait()
        if part + 2 < parts:
            load(part + 2).start()
        if part > 1:
            save(part - 2).wait()

        def some(h, _):
            for u in range(4):
                k = h * 4 + u
                data = buffer[part % 3, k].astype(F32)
                for j in range(8):
                    turned[u, pl.ds(j, 8, stride=8), :] = data[:, j * LANES : (j + 1) * LANES]
            for u in range(4):
                result[part % 2, h * 4 + u] = turned[u].astype(BF16)
            return 0

        lax.fori_loop(0, size // 4, some, 0)
        if part > 0 and starts[part] < starts[part - 1] + size:
            save(part - 1).wait()
            save(part).start()
            save(part).wait()
        else:
            save(part).start()
    overlap = parts > 1 and starts[-1] < starts[-2] + size
    if not overlap:
        if parts > 1:
            save(parts - 2).wait()
        save(parts - 1).wait()


def cos_sin_turns(x):
    x = x - jnp.round(x)
    quarter = jnp.round(x * 4.0)
    y = (x - quarter * 0.25) * (2.0 * math.pi)
    z = y * y
    s = y * (1.0 + z * (-1.0 / 6 + z * (1.0 / 120 + z * (-1.0 / 5040 + z * (1.0 / 362880)))))
    c = 1.0 + z * (-0.5 + z * (1.0 / 24 + z * (-1.0 / 720 + z * (1.0 / 40320 + z * (-1.0 / 3628800)))))
    odd = jnp.abs(quarter) == 1.0
    negative_c = (quarter == 1.0) | (jnp.abs(quarter) == 2.0)
    negative_s = (quarter == -1.0) | (jnp.abs(quarter) == 2.0)
    cos = jnp.where(odd, s, c)
    sin = jnp.where(odd, c, s)
    return jnp.where(negative_c, -cos, cos), jnp.where(negative_s, -sin, sin)


def cmul(a, b):
    return a[0] * b[0] - a[1] * b[1], a[0] * b[1] + a[1] * b[0]


def conj(a):
    return a[0], -a[1]


def both(a, b):
    rr, ii, ri, ir = a[0] * b[0], a[1] * b[1], a[0] * b[1], a[1] * b[0]
    return (rr - ii, ri + ir), (rr + ii, ir - ri)


def split(x):
    high = x.astype(BF16)
    return high, (x - high.astype(F32)).astype(BF16)


def main_kernel(
    slots, intervals, recv, freq_hbm, inner_hbm, twiddle_hbm, outer_hbm, planes,
    strip,
    meta, index, table, sky, screen, acc, place, freq, inner, twiddle, outer,
    index_sem, screen_sems, table_sems,
):
    peers, rows, _ = recv.shape
    most = meta.shape[0]
    tiles = strip.shape[2] // LANES
    lane = lax.broadcasted_iota(jnp.int32, (8, LANES), 1)
    step = (lane // (LANES // NT)).astype(F32)

    tables = [
        pltpu.make_async_copy(source, target, table_sems.at[k])
        for k, (source, target) in enumerate(
            ((freq_hbm, freq), (inner_hbm, inner), (twiddle_hbm, twiddle), (outer_hbm, outer))
        )
    ]
    for copy in tables:
        copy.start()

    halves = -(-slots // 8)
    sublane = lax.broadcasted_iota(jnp.int32, (8, LANES), 0)
    records = []
    for t in range(peers):
        chunk = recv[t, slots * 8 : slots * 8 + 8, :].astype(F32)
        for h in range(halves):
            record = pltpu.roll(chunk, LANES // 2, 1) if h else chunk
            record = jnp.where(lane == 7, float(t), record)
            records.append(jnp.where(lane == 8, (sublane + 8 * h).astype(F32), record))
    records = jnp.concatenate(records, axis=0)
    many = records.shape[0]
    filled = (records[:, 6:7] > 0.0).astype(F32)
    flags = jnp.where(lax.broadcasted_iota(jnp.int32, (many, LANES), 1) == 0, filled, 0.0).astype(BF16)
    dims = (((1,), (1,)), ((), ()))
    used = lax.dot_general(jnp.ones((8, LANES), BF16), flags, dims, preferred_element_type=F32)
    before = lax.broadcasted_iota(jnp.int32, (many, many), 0) < lax.broadcasted_iota(jnp.int32, (many, many), 1)
    rank = jnp.dot(used.astype(BF16), before.astype(F32).astype(BF16), preferred_element_type=F32)
    order = lax.broadcasted_iota(jnp.int32, (most, many), 0).astype(F32)
    pick = jnp.where((rank[0:1] == order) & (used[0:1] > 0.5), 1.0, 0.0)
    m = jnp.dot(pick.astype(BF16), records.astype(BF16), preferred_element_type=F32)
    meta[...] = m
    number = jnp.sum(filled).astype(jnp.int32)
    groups = jnp.maximum((number + 15) // 16, 1)

    field = lax.broadcasted_iota(jnp.int32, (8, LANES), 0)
    pickers = jnp.zeros((8, LANES), F32)
    for f, source in enumerate((0, 1, 3, 4, 5, 7, 8, 9)):
        pickers = jnp.where((field == f) & (lane == source), 1.0, pickers)
    width = index.shape[1]
    wide = m.astype(BF16)
    if width > most:
        wide = jnp.concatenate([wide, jnp.zeros((width - most, LANES), BF16)], axis=0)
    fields = lax.dot_general(pickers.astype(BF16), wide, dims, preferred_element_type=F32)
    index[...] = fields.astype(jnp.int32)
    to_scalar = pltpu.make_async_copy(index, place, index_sem)
    to_scalar.start()

    tables[0].wait()

    channel = jnp.concatenate([freq[...], freq[...]], axis=1)

    def phases(g):
        here = meta[pl.ds(pl.multiple_of(g * 8, 8), 8), :]
        start = here[:, 2:3] * NT
        live = (step < here[:, 6:7]).astype(F32)
        x, y, z = [sum(here[:, 16 + 3 * a + k : 17 + 3 * a + k] for k in range(3)) for a in range(3)]
        scale = hour_step / (2.0 * math.pi)
        cos_now, sin_now = cos_sin_turns(scale * (start + step))
        cos_mid, sin_mid = cos_sin_turns(scale * (start + 0.5 * (NT - 1) + 0.0 * step))

        def track(c, s):
            u = s * x + c * y
            v = (-math.sin(declination)) * c * x + math.sin(declination) * s * y + math.cos(declination) * z
            return u, v

        u_now, v_now = track(cos_now, sin_now)
        u_mid, v_mid = track(cos_mid, sin_mid)
        du = (u_now * channel - u_mid) * (1.0 / SUB)
        dv = (v_now * channel - v_mid) * (1.0 / SUB)
        e1 = cos_sin_turns(0.5 * du)
        e2 = cmul(e1, e1)
        e3 = cmul(e2, e1)
        e4 = cmul(e2, e2)
        e8 = cmul(e4, e4)
        g1 = cos_sin_turns(dv)
        g2 = cmul(g1, g1)
        g3 = cmul(g2, g1)
        g4 = cmul(g2, g2)
        g8 = cmul(g4, g4)
        g12 = cmul(g8, g4)
        mid = (e3[0] * live, e3[1] * live)
        ups = [mid]
        for _ in range(3):
            ups.append(cmul(ups[-1], e8))
        downs = [cmul(mid, conj(e8))]
        for _ in range(3):
            downs.append(cmul(downs[-1], conj(e8)))
        row_phase = downs[::-1] + ups
        ones = (jnp.ones_like(du), jnp.zeros_like(du))
        col_phase = [conj(g4), conj(g3), conj(g2), conj(g1), ones, g1, g2, g3]
        base = pl.multiple_of(g * (KINDS * 8), 8)

        def put(kind, value):
            table[pl.ds(base + kind * 8, 8), :] = value

        for k in range(8):
            put(k, row_phase[k][0])
            put(8 + k, row_phase[k][1])
            put(16 + k, col_phase[k][0])
            put(24 + k, col_phase[k][1])
        k = 32
        for e in (e1, e3):
            plus12, minus12 = both(e, g12)
            plus4, minus4 = both(e, g4)
            for value in (minus12, minus4, plus4, plus12):
                put(k, value[0])
                put(k + 8, value[1])
                k += 1

    def all_phases(g, _):
        for h in range(2):
            phases(g * 2 + h)
        return 0


    def image(g, u):
        n = g * 16 + u
        base = (2 * g + u // 8) * (KINDS * 8) + u % 8

        def rows_of(kind):
            return table[pl.ds(base + kind * 8, 8, stride=8), :]

        def row_of(kind):
            return table[pl.ds(base + kind * 8, 1), :]

        row_phase = (rows_of(0), rows_of(8))
        col_phase = (rows_of(16), rows_of(24))
        cells = [[None] * 4 for _ in range(4)]
        for k in range(8):
            mi, bb = k // 4, k % 4
            plus, minus = both(col_phase, (row_of(32 + k), row_of(40 + k)))
            cells[2 + mi][bb] = plus
            cells[1 - mi][3 - bb] = minus
        real = jnp.concatenate([cells[a][b][0] for a in range(4) for b in range(4)], axis=0)
        imag = jnp.concatenate([cells[a][b][1] for a in range(4) for b in range(4)], axis=0)
        right = jnp.concatenate([real.astype(BF16), imag.astype(BF16)], axis=1)
        block = recv[place[5, n], pl.ds(pl.multiple_of(place[6, n] * 8, 8), 8), :].astype(F32)
        reals, imags = [], []
        for p in range(4):
            value = cmul(row_phase, (block[2 * p : 2 * p + 1, :], block[2 * p + 1 : 2 * p + 2, :]))
            reals.append(value[0])
            imags.append(value[1])
        real = jnp.concatenate(reals, axis=0)
        imag = jnp.concatenate(imags, axis=0)
        left = jnp.concatenate(
            [jnp.concatenate([real, -imag], axis=1), jnp.concatenate([imag, real], axis=1)], axis=0
        )
        sky[n] = lax.dot_general(left.astype(BF16), right, dims, preferred_element_type=F32)

    batch = 16

    def images(g):
        for u in range(batch):
            image(g, u)

    def fetch(g, way):
        for u in range(batch):
            for side in range(2):
                n = g * batch + u
                source = planes.at[place[side, n] * intervals + place[7, n]]
                pltpu.make_async_copy(source, screen.at[2 * n + side], screen_sems.at[way]).start()

    def land(g, way):
        here = screen.at[pl.ds(g * 2 * batch, 2 * batch)]
        pltpu.make_async_copy(planes.at[pl.ds(0, 2 * batch)], here, screen_sems.at[way]).wait()

    all_phases(0, 0)
    acc[:, :, STRIP : 2 * STRIP, :] = jnp.zeros((2 * tiles, 8, STRIP, LANES), F32)
    to_scalar.wait()
    fetch(0, 0)
    lax.fori_loop(1, groups, all_phases, 0)
    images(0)
    for copy in tables[1:]:
        copy.wait()

    def settle(g, size, ahead):
        results = []
        for u in range(size):
            n = g * batch + u
            jones = []
            for side in range(2):
                entry = [screen[2 * n + side, 16 * k : 16 * k + 16, :].astype(F32) for k in range(4)]
                jones.append([(e[:8], e[8:]) for e in entry])
            image = sky[n]
            value = [(image[8 * p : 8 * p + 8], image[32 + 8 * p : 40 + 8 * p]) for p in range(4)]
            left, right = jones

            def add(a, b):
                return a[0] + b[0], a[1] + b[1]

            mixed = [
                add(cmul(left[2 * i], value[k]), cmul(left[2 * i + 1], value[2 + k]))
                for i in range(2)
                for k in range(2)
            ]
            corrected = [
                add(cmul(mixed[2 * i], conj(right[2 * j])), cmul(mixed[2 * i + 1], conj(right[2 * j + 1])))
                for i in range(2)
                for j in range(2)
            ]
            stacked = jnp.concatenate([c[0] for c in corrected] + [c[1] for c in corrected], axis=0)
            high, low = split(stacked)
            turned = jnp.dot(inner[...], jnp.concatenate([high, low], axis=0), preferred_element_type=F32)
            tw = (twiddle[0], twiddle[1])
            spun = [cmul((turned[8 * p : 8 * p + 8], turned[32 + 8 * p : 40 + 8 * p]), tw) for p in range(4)]
            results.append(
                jnp.concatenate(
                    [jnp.concatenate([s[0] for s in spun], axis=0), jnp.concatenate([s[1] for s in spun], axis=0)],
                    axis=1,
                )
            )
        high, low = split(jnp.concatenate(results, axis=0))
        out = jnp.dot(high, outer[0], preferred_element_type=F32)
        out += jnp.dot(high, outer[1], preferred_element_type=F32)
        out += jnp.dot(low, outer[0], preferred_element_type=F32)
        if ahead is not None:
            images(ahead)
        for u in range(size):
            n = g * batch + u
            first = place[2, n]
            tile = place[3, n]
            shift = place[4, n]
            inside = (lane >= shift) & (lane < shift + SUB)
            cells = []
            for p in range(4):
                for r in range(2):
                    cell = out[u * 32 + 8 * p : u * 32 + 8 * p + 8, r * LANES : (r + 1) * LANES]
                    parts = []
                    for k4 in range(4):
                        turn = (shift + (LANES - SUB * k4)) % LANES
                        parts.append(jnp.where(inside, pltpu.roll(cell, turn, 1), 0.0))
                    cells.append(jnp.concatenate(parts, axis=0))
            spot = (tile, slice(None), pl.ds(first, SUB), slice(None))
            acc[spot] = acc[spot] + jnp.stack(cells)

    def grid(g, _):
        land(g, g % 2)
        fetch(g + 1, 1 - g % 2)
        settle(g, batch, g + 1)
        return 0

    end = groups - 1
    lax.fori_loop(0, end, grid, 0)
    land(end, end % 2)
    few = number - end * batch <= batch // 2

    @pl.when(few)
    def _():
        settle(end, batch // 2, None)

    @pl.when(jnp.logical_not(few))
    def _():
        settle(end, batch, None)


    half = lax.broadcasted_iota(jnp.int32, (STRIP, LANES), 1) < LANES // 2
    mine = slice(STRIP, 2 * STRIP)
    for plane_at in range(8):
        behind = None
        for t in range(tiles):
            value = acc[1 + t, plane_at, mine, :]
            turned = None
            if t < tiles - 1:
                turned = pltpu.roll(acc[1 + tiles + t, plane_at, mine, :], LANES // 2, 1)
                value = value + jnp.where(half, 0.0, turned)
            if behind is not None:
                value = value + jnp.where(half, behind, 0.0)
            behind = turned
            strip[plane_at, :, t * LANES : (t + 1) * LANES] = value


def body(visibilities, screens, positions, channel_freq, owner, baseline, tick, row, col, steps):
    peers = lax.axis_size("tile")
    items = visibilities.shape[0]
    slots = 3 * max(2, 2 * items // peers)
    rows = slots * 8 + 8
    most = -(-peers * slots // 8) * 8
    wide = -(-most // LANES) * LANES
    columns = GCOLS
    tiles = columns // LANES

    intervals = screens.shape[1]
    packed = pl.pallas_call(
        functools.partial(pack_kernel, slots, intervals, columns),
        out_shape=jax.ShapeDtypeStruct((peers, rows, LANES), BF16),
        in_specs=[SMEM] * 2 + [VMEM] * 6,
        out_specs=VMEM,
        scratch_shapes=[
            pltpu.VMEM(((peers + 1) * rows, LANES), F32),
            pltpu.VMEM(((peers + 1) * 16, LANES), F32),
            pltpu.VMEM((items, LANES), F32),
            pltpu.SMEM((peers + 1,), jnp.int32),
        ],
        name="pack",
    )(owner[:, 0], row, baseline[None], tick[None], col[None], steps[None], positions.T, visibilities)
    received = lax.all_to_all(packed, "tile", split_axis=0, concat_axis=0, tiled=True)

    table = screens.reshape(screens.shape[0] * screens.shape[1], 8, SUB * SUB)
    total = table.shape[0]
    size = 40
    planes = pl.pallas_call(
        planes_kernel,
        out_shape=jax.ShapeDtypeStruct((total, 64, LANES), BF16),
        in_specs=[ANY],
        out_specs=ANY,
        scratch_shapes=[
            pltpu.VMEM((3, size, 8, SUB * SUB), BF16),
            pltpu.VMEM((4, 64, LANES), F32),
            pltpu.VMEM((2, size, 64, LANES), BF16),
            pltpu.SemaphoreType.DMA((3,)),
            pltpu.SemaphoreType.DMA((2,)),
        ],
        cost_estimate=pl.CostEstimate(flops=10**8, bytes_accessed=3 * 10**7, transcendentals=0),
        compiler_params=pltpu.CompilerParams(vmem_limit_bytes=56 * 1024 * 1024),
        name="screen_planes",
    )(table)

    inner, twiddle, outer = dft_tables()
    return pl.pallas_call(
        functools.partial(main_kernel, slots, intervals),
        out_shape=jax.ShapeDtypeStruct((8, STRIP, columns), F32),
        in_specs=[VMEM] + [ANY] * 5,
        out_specs=VMEM,
        scratch_shapes=[
            pltpu.VMEM((most, LANES), F32),
            pltpu.VMEM((8, wide), jnp.int32),
            pltpu.VMEM((most * KINDS, LANES), F32),
            pltpu.VMEM((most, 64, LANES), F32),
            pltpu.VMEM((2 * most, 64, LANES), BF16),
            pltpu.VMEM((2 * tiles, 8, 3 * STRIP, LANES), F32),
            pltpu.SMEM((8, wide), jnp.int32),
            pltpu.VMEM((1, channel_freq.shape[0]), F32),
            pltpu.VMEM(inner.shape, inner.dtype),
            pltpu.VMEM(twiddle.shape, twiddle.dtype),
            pltpu.VMEM(outer.shape, outer.dtype),
            pltpu.SemaphoreType.DMA,
            pltpu.SemaphoreType.DMA((2,)),
            pltpu.SemaphoreType.DMA((4,)),
        ],
        compiler_params=pltpu.CompilerParams(vmem_limit_bytes=50 * 1024 * 1024),
        name="grid_items",
    )(received, channel_freq[None, :], inner, twiddle, outer, planes)


def solution(mesh):
    return jax.shard_map(
        body,
        mesh=mesh,
        in_specs=(
            P(("band", "tile"), None, None),
            P("band", None, None, None),
            P(),
            P("band"),
            P(("band", "tile"), None),
            P(("band", "tile")),
            P(("band", "tile")),
            P(("band", "tile")),
            P(("band", "tile")),
            P(("band", "tile")),
        ),
        out_specs=P("band", "tile", None),
        check_vma=False,
    )
```
